32 devices in a mesh: group: 2 (over x), lat: 8 (over z, y), spec: 2 (over core).
Axes of the slice: x: 2, y: 2, z: 4, core: 2. Of those that a mesh axis runs over, the one named last changes fastest.
Arguments:
- field_grid: float32 [2, 32, 64, 3600], P(None, 'lat', ('group', 'spec')), parts along dimension 2, may hold values from -6 to 6
- quad_weight: float32 [32], P('lat'), may hold values from 0.5 to 2
- owner_waves: int32 [2, 8, 2], replicated, may hold values from 0 to 1800, as said below
- skip_blocks: int32 [8, 2, 8, 2], replicated, may hold values from 0 to 3
- legendre_table: bfloat16 [2, 8, 30, 32, 64], P('spec', None, None, 'lat'), may hold values from -24 to 24
- given_spectrum: bfloat16 [2, 8, 30, 2, 64, 64], P('spec', 'lat', None, None, 'group'), parts along dimension 4, may hold values from -6 to 6
Outputs:
- spectrum: float32 [2, 8, 30, 2, 64, 64], P('spec', 'lat', None, None, 'group'), parts along dimension 4
- back_grid: float32 [2, 32, 64, 3600], P(None, 'lat', ('group', 'spec')), parts along dimension 2
The draws below stay inside these ranges and needn't reach their ends.
There are 2 independent parts, one for each index of `group`. The reference program is written for one: setup_inputs(seed, part) draws one part's arguments, and reference() takes and returns one part's arrays. A program takes and returns all parts, laid end to end along the dimension named above; an argument that names none is the same for every part. Nothing has to cross between parts.
Inputs may be any that keep to these rules, and one draw needn't show every extreme that they name: `owner_waves`: row (h, o) holds a wavenumber m below 900 and then its partner 1800 - m; all wavenumbers are distinct, and 0 and 1800 are among them.
All inputs are finite; a program needn't handle non-finite values.
Results may differ from the reference program's by a relative error of at most 0.0029.
Values may be sent and summed in bfloat16 or wider, within the bound.
A program may use at most 256 MiB of HBM per device.

```python
import math
import jax
import jax.numpy as jnp
from jax import lax

C = 32
L = 1800
NLON = 3600
KB = 64
PAIR_DEV = 4
NPAIR = 32
M_WIN = 32
OWN_BLK = 30
N_LAT = 8
N_SPEC = 2


def draw_owner_waves(key, part):
    key = jax.random.fold_in(key, 7)
    first_key, second_key = jax.random.split(key)
    lower_count = M_WIN // 2
    others = jax.random.permutation(first_key, L // 2 - 1)[:lower_count - 1].astype(jnp.int32) + 1
    lower_waves = jnp.concatenate([jnp.zeros((1,), jnp.int32), others])
    shuffle_order = jax.random.permutation(second_key, lower_count)
    lower_waves = lower_waves[shuffle_order]
    return jnp.stack([lower_waves, L - lower_waves], axis=1).reshape(N_SPEC, N_LAT, 2)


def plant(array, rng, smallest, high):
    longest = array.shape.index(max(array.shape))
    spots = []
    for shift in (0, 1):
        where = [jax.random.randint(jax.random.fold_in(rng, axis), (), 0, length) for axis, length in enumerate(array.shape)]
        where[longest] = (where[longest] + shift) % array.shape[longest]
        spots.append(tuple(where))
    return array.at[spots[0]].set(smallest).at[spots[1]].set(high)


def level_of(rng, extent, cuts, smallest, largest):
    loudness, own = 1.0, jax.random.fold_in(rng, 6)
    for axis_at, shards_of in cuts:
        steps = jnp.exp(jax.random.uniform(jax.random.fold_in(own, axis_at), (shards_of,), jnp.float32, smallest / len(cuts), largest / len(cuts)))
        loudness = loudness * jnp.repeat(steps, extent[axis_at] // shards_of).reshape([-1 if axis == axis_at else 1 for axis in range(len(extent))])
    return loudness


def normal_values(key, extent, deviation, limit, cuts=(), held_as=jnp.bfloat16):
    drawn = jax.random.normal(key, extent, jnp.float32) * deviation
    if len(cuts) > 0:
        drawn = level_of(key, extent, cuts, -0.22, 0.18) * drawn
    return jnp.clip(drawn, min=-limit, max=limit).astype(held_as)


def setup_inputs(seed: int = 0, part: int = 0) -> dict:
    keys = jax.random.split(jax.random.key(seed), 7)
    part_keys = jax.random.split(jax.random.fold_in(keys[6], part), 7)
    field_grid = normal_values(part_keys[0], (2, NPAIR, C, NLON), 1.0, 6.0, ((1, 8), (2, 2)), jnp.float32)
    quad_weight = jnp.clip(jnp.exp(math.log(2.0) - 1.3862944 * jax.random.uniform(keys[1], (NPAIR,), jnp.float32) ** level_of(keys[1], (NPAIR,), ((0, 8),), -0.2, 0.2)), 0.5, 2.0)
    owner_waves = draw_owner_waves(jax.random.fold_in(keys[6], 71), part)
    skip_blocks = plant(jax.random.randint(keys[3], (N_LAT, N_SPEC, N_LAT, 2), 0, 4), jax.random.fold_in(keys[3], 1), 0, 3).astype(jnp.int32)
    legendre_table = normal_values(keys[4], (N_SPEC, N_LAT, OWN_BLK, NPAIR, KB), 4.0, 24.0, ((0, 2), (3, 8)))
    given_spectrum = normal_values(part_keys[5], (N_SPEC, N_LAT, OWN_BLK, 2, C, KB), 1.0, 6.0, ((0, 2), (1, 8)))
    return {"field_grid": field_grid, "quad_weight": quad_weight, "owner_waves": owner_waves, "skip_blocks": skip_blocks, "legendre_table": legendre_table, "given_spectrum": given_spectrum}


def fourier_table(owner_waves, length):
    wave_list = owner_waves.reshape(-1)
    grid_points = jnp.arange(length, dtype=jnp.int32)
    phase_index = (grid_points[:, None] * wave_list[None, :]) % length
    angles = phase_index.astype(jnp.float32) * (2.0 * math.pi / length)
    return jnp.concatenate([jnp.cos(angles), -jnp.sin(angles)], axis=1)


def legendre_mask(block_table, pair_waves, pair_skip):
    block_counts = (L + KB - pair_waves) // KB
    slot_index = jnp.arange(block_table.shape[1], dtype=jnp.int32)
    slot_start = jnp.stack([jnp.zeros_like(block_counts[:, 0]), block_counts[:, 0]], axis=1)
    block_index = slot_index[None, :, None] - slot_start[:, None, :]
    inside = (block_index >= 0) & (block_index < block_counts[:, None, :])
    degree = pair_waves[:, None, :, None] + KB * block_index[:, :, :, None] + jnp.arange(KB, dtype=jnp.int32)
    inside = inside[:, :, :, None] & (degree <= L)
    not_skipped = block_index[:, :, :, None] >= jnp.transpose(pair_skip, (1, 2, 0))[:, None, :, :]
    keep_mask = inside[:, :, :, None, :] & not_skipped[:, :, :, :, None]
    return jnp.where(keep_mask, block_table[:, :, None, :, :], jnp.zeros((), block_table.dtype))


def spread_parity(folded, degrees):
    parity = (jnp.arange(degrees, dtype=jnp.int32) % 2)[None, None, None, :, None, None]
    even_part = folded[:, :, :, 0][:, :, :, None]
    odd_part = folded[:, :, :, 1][:, :, :, None]
    return jnp.where(parity == 0, even_part, odd_part)


def forward_terms(masked, folded):
    degree_fold = spread_parity(folded, masked.shape[4])
    return jnp.einsum("nksji,jnsirc->nkrci", masked, degree_fold, preferred_element_type=jnp.float32)


def adjoint_terms(masked, coeffs):
    per_degree = jnp.einsum("nksji,nkrci->jnsirc", masked, coeffs, preferred_element_type=jnp.float32)
    shape_now = per_degree.shape
    split_degree = per_degree.reshape(shape_now[:3] + (shape_now[3] // 2, 2) + shape_now[4:])
    return jnp.sum(split_degree, axis=3)


def fold_forward(fourier, quad_weight):
    symmetric = fourier[0] + fourier[1]
    antisymmetric = fourier[0] - fourier[1]
    stacked = jnp.stack([symmetric, antisymmetric], axis=-1) * quad_weight[:, None, None, None, None]
    stacked = stacked.astype(jnp.bfloat16)
    pair_count, channels, part_count, wave_count, parity = stacked.shape
    shaped = stacked.reshape(pair_count, channels, part_count, wave_count // 2, 2, parity)
    return jnp.transpose(shaped, (0, 3, 4, 5, 2, 1))


def fold_adjoint(synthesis, quad_weight):
    north_part = synthesis[:, :, :, 0] + synthesis[:, :, :, 1]
    south_part = synthesis[:, :, :, 0] - synthesis[:, :, :, 1]
    stacked = jnp.stack([north_part, south_part], axis=0) * quad_weight[None, :, None, None, None, None]
    hemispheres, pair_count, owner_count, slots_two, part_count, channels = stacked.shape
    moved = jnp.transpose(stacked, (0, 1, 5, 4, 2, 3))
    return moved.reshape(hemispheres, pair_count, channels, part_count, owner_count * slots_two)


def reference(field_grid, quad_weight, owner_waves, skip_blocks, legendre_table, given_spectrum):
    length = NLON
    wave_table = fourier_table(owner_waves, length)
    flat_rows = field_grid.reshape(-1, length)
    fourier = jnp.dot(flat_rows, wave_table, precision=lax.Precision.HIGHEST, preferred_element_type=jnp.float32) * (1.0 / length)
    fourier = fourier.reshape(2, NPAIR, C, 2, M_WIN)
    folded = fold_forward(fourier, quad_weight)
    folded = folded.reshape(NPAIR, N_SPEC, N_LAT, 2, 2, 2, C)
    spectra = []
    syntheses = []
    for spec_index in range(N_SPEC):
        skip_rows = jnp.repeat(skip_blocks[:, spec_index], PAIR_DEV, axis=0)
        masked = legendre_mask(legendre_table[spec_index], owner_waves[spec_index], skip_rows).astype(jnp.float32)
        own_fold = folded[:, spec_index].astype(jnp.float32)
        spectra.append(forward_terms(masked, own_fold))
        syntheses.append(adjoint_terms(masked, given_spectrum[spec_index].astype(jnp.float32)))
    spectrum = jnp.stack(spectra, axis=0)
    synthesis = jnp.concatenate(syntheses, axis=1)
    back_fourier = fold_adjoint(synthesis, quad_weight)
    back_rows = back_fourier.reshape(-1, 2 * M_WIN)
    back_grid = jnp.dot(back_rows, wave_table.T, precision=lax.Precision.HIGHEST, preferred_element_type=jnp.float32) * (1.0 / length)
    return spectrum, back_grid.reshape(2, NPAIR, C, NLON)
```

```python
import math

import jax
import jax.numpy as jnp
from jax import lax
from jax.sharding import PartitionSpec as P

L = 1800
KB = 64


def fourier_table(owner_waves, length):
    wave_list = owner_waves.reshape(-1)
    grid_points = jnp.arange(length, dtype=jnp.int32)
    phase_index = grid_points[:, None] * wave_list[None, :] % length
    angles = phase_index.astype(jnp.float32) * (2.0 * math.pi / length)
    return jnp.concatenate([jnp.cos(angles), -jnp.sin(angles)], axis=1)


def owner_table(blocks, waves, skips, pair_dev):
    slots, pairs, degrees = blocks.shape
    counts = (L + KB - waves) // KB
    starts = jnp.stack([jnp.zeros_like(counts[0]), counts[0]])
    block = jnp.arange(slots, dtype=jnp.int32)[None, :] - starts[:, None]
    inside = (block >= 0) & (block < counts[:, None])
    ramp = jnp.arange(degrees, dtype=jnp.int32)
    inside = inside[:, :, None] & (waves[:, None, None] + KB * block[:, :, None] + ramp <= L)
    skip_rows = jnp.repeat(skips.T, pair_dev, axis=1)
    stored = block[:, None, :] >= skip_rows[:, :, None]
    keep = inside[:, None, None] & stored[:, :, None, :, None]
    keep = keep & (ramp % 2 == jnp.arange(2)[:, None])[None, None, :, None, :]
    moved = jnp.transpose(blocks, (1, 0, 2))[None, :, None]
    return jnp.where(keep, moved, jnp.zeros((), blocks.dtype))


def on_device(
    lat_count, spec_count, field_grid, quad_weight, owner_waves, skip_blocks, legendre_table, given_spectrum
):
    hemispheres, pair_dev, channels, length = field_grid.shape
    table_blocks = lax.all_to_all(legendre_table[0], "lat", split_axis=0, concat_axis=2, tiled=True)[0]
    wave_table = fourier_table(owner_waves, length)
    wave_count = wave_table.shape[1] // 2
    fourier = jnp.dot(
        field_grid.reshape(-1, length),
        wave_table,
        precision=lax.Precision.HIGHEST,
        preferred_element_type=jnp.float32,
    ) * (1.0 / length)
    fourier = fourier.reshape(hemispheres, pair_dev, channels, 2, wave_count)
    weight = quad_weight[:, None, None, None]
    folded = jnp.stack(
        [(fourier[0] + fourier[1]) * weight, (fourier[0] - fourier[1]) * weight], axis=1
    ).astype(jnp.bfloat16)
    folded = folded.reshape(pair_dev, 2, channels, 2, wave_count // 2, 2)
    folded = jnp.transpose(folded, (4, 0, 5, 1, 3, 2))
    folded = lax.all_to_all(folded, ("spec", "lat"), split_axis=0, concat_axis=0, tiled=True)
    folded = folded.reshape(spec_count, lat_count, pair_dev, 2, 2, 2, channels)
    folded = jnp.transpose(folded, (3, 1, 2, 4, 5, 0, 6))
    rows = 2 * lat_count * pair_dev * 2
    columns = 2 * spec_count * channels
    folded = folded.reshape(rows, columns)

    spec_index = lax.axis_index("spec")
    lat_index = lax.axis_index("lat")
    waves = owner_waves[spec_index, lat_index]
    skips = skip_blocks[:, spec_index, lat_index]
    masked = owner_table(table_blocks, waves, skips, pair_dev)
    masked = masked.reshape((rows,) + masked.shape[3:])
    coeffs = given_spectrum[0, 0].reshape(given_spectrum.shape[2], columns, KB)
    synthesis = jnp.einsum("qki,kxi->qx", masked, coeffs, preferred_element_type=jnp.float32)
    spectrum = jnp.einsum("qki,qx->kxi", masked, folded, preferred_element_type=jnp.float32)

    synthesis = synthesis.reshape(2, lat_count, pair_dev, 2, 2, spec_count, channels)
    synthesis = jnp.transpose(synthesis, (5, 1, 2, 0, 3, 4, 6)).reshape(
        spec_count * lat_count, pair_dev, 2, 2, 2, channels
    )
    synthesis = lax.all_to_all(synthesis, ("spec", "lat"), split_axis=0, concat_axis=0, tiled=True)
    back = jnp.stack(
        [synthesis[:, :, :, 0] + synthesis[:, :, :, 1], synthesis[:, :, :, 0] - synthesis[:, :, :, 1]]
    ) * quad_weight[None, None, :, None, None, None]
    back = jnp.transpose(back, (0, 2, 5, 4, 1, 3)).reshape(-1, 2 * wave_count)
    back_grid = jnp.dot(
        back, wave_table.T, precision=lax.Precision.HIGHEST, preferred_element_type=jnp.float32
    ) * (1.0 / length)
    return (spectrum.reshape(given_spectrum.shape), back_grid.reshape(field_grid.shape))


def solution(mesh):
    lat_count, spec_count = mesh.shape["lat"], mesh.shape["spec"]

    def body(*args):
        return on_device(lat_count, spec_count, *args)

    return jax.shard_map(
        body,
        mesh=mesh,
        in_specs=(
            P(None, "lat", ("group", "spec"), None),
            P("lat"),
            P(),
            P(),
            P("spec", None, None, "lat", None),
            P("spec", "lat", None, None, "group", None),
        ),
        out_specs=(
            P("spec", "lat", None, None, "group", None),
            P(None, "lat", ("group", "spec"), None),
        ),
        check_vma=False,
    )
```

```python
import functools
import math

import jax
import jax.numpy as jnp
from jax import lax
from jax.experimental import pallas as pl
from jax.experimental.pallas import tpu as pltpu
from jax.sharding import PartitionSpec as P

L = 1800
KB = 64
SHIFT = 6
LANES = 128
WIDE = 512
MESH = pl.DeviceIdType.MESH
ACROSS = (((1,), (1,)), ((), ()))
PLAIN = (((1,), (0,)), ((), ()))


def dot(a, b, dims=PLAIN):
    return lax.dot_general(a, b, dims, preferred_element_type=jnp.float32)


def cosine(phase, length):
    turns = jnp.floor(phase * (1.0 / length) + 0.5)
    angle = (phase - turns * length) * (2.0 * math.pi / length)
    z = angle * angle
    total = jnp.full_like(z, 1.0 / math.factorial(20))
    for n in range(18, -1, -2):
        sign = -1.0 if (n // 2) % 2 else 1.0
        total = total * z + sign / math.factorial(n)
    return total


def split(value):
    high = value.astype(jnp.bfloat16)
    return high, (value - high.astype(jnp.float32)).astype(jnp.bfloat16)


def kernel(
    lat_count,
    spec_count,
    waves_ref,
    skip_ref,
    weight_ref,
    field_ref,
    table_ref,
    given_ref,
    spectrum_ref,
    grid_ref,
    field_buf,
    table_recv,
    stage,
    fold_send,
    fold_recv,
    syn_send,
    syn_recv,
    waves8,
    masked,
    coeffs,
    field_sem,
    table_send_sem,
    table_recv_sem,
    fold_send_sem,
    fold_recv_sem,
    syn_send_sem,
    syn_recv_sem,
):
    f32, bf16 = jnp.float32, jnp.bfloat16
    length = field_ref.shape[1]
    pair_dev = weight_ref.shape[0]
    channels = LANES // (2 * pair_dev)
    slots = given_ref.shape[0]
    columns = given_ref.shape[1]
    dest_count = lat_count * spec_count
    half = 2 * dest_count
    group = 4 * pair_dev
    lat = lax.axis_index("lat")
    spec = lax.axis_index("spec")
    me = spec * lat_count + lat

    def place(t, n, mine):
        return lax.rem(mine + t, n)

    def device(d):
        return {"spec": d // lat_count, "lat": lax.rem(d, lat_count)}

    field_copy = pltpu.make_async_copy(field_ref, field_buf, field_sem)
    field_copy.start()
    barrier = pltpu.get_barrier_semaphore()

    @pl.loop(1, dest_count)
    def _(t):
        pl.semaphore_signal(
            barrier, inc=1, device_id=device(place(t, dest_count, me)), device_id_type=MESH
        )

    pl.semaphore_wait(barrier, dest_count - 1)

    def table_copy(to, slot):
        return pltpu.make_async_remote_copy(
            src_ref=table_ref.at[pl.ds(to * 16, 16)],
            dst_ref=table_recv.at[pl.ds(slot * 16, 16)],
            send_sem=table_send_sem.at[to],
            recv_sem=table_recv_sem.at[slot],
            device_id={"lat": to},
            device_id_type=MESH,
        )

    def fold_copy(to, from_spec, from_lat):
        return pltpu.make_async_remote_copy(
            src_ref=fold_send.at[pl.ds(to * 16, 16)],
            dst_ref=fold_recv.at[from_spec, pl.ds(from_lat * 16, 16)],
            send_sem=fold_send_sem.at[to],
            recv_sem=fold_recv_sem.at[from_spec * lat_count + from_lat],
            device_id=device(to),
            device_id_type=MESH,
        )

    def syn_copy(to, slot):
        return pltpu.make_async_remote_copy(
            src_ref=syn_send.at[pl.ds(lax.rem(to, lat_count) * 16, 16)],
            dst_ref=syn_recv.at[pl.ds(slot * 16, 16)],
            send_sem=syn_send_sem.at[to],
            recv_sem=syn_recv_sem.at[slot],
            device_id=device(to),
            device_id_type=MESH,
        )

    @pl.loop(1, lat_count)
    def _(t):
        table_copy(place(t, lat_count, lat), lat).start()

    own = pl.ds(pl.multiple_of(lat * 16, 16), 16)
    table_recv[own, :] = table_ref[own, :]

    row8 = lax.broadcasted_iota(jnp.int32, (8, LANES), 0)
    tiles = []
    for tile in range(half // 8):
        wave = jnp.zeros((8, LANES), jnp.int32)
        for row in range(8):
            d, s = divmod(tile * 8 + row, 2)
            wave = jnp.where(row8 == row, waves_ref[d // lat_count, s, d % lat_count], wave)
        tiles.append(wave)
    wave = jnp.concatenate(tiles, axis=0).astype(f32)
    lane_half = lax.broadcasted_iota(jnp.int32, (half, LANES), 1).astype(f32)
    fine = wave * lane_half
    coarse = wave * (lane_half * LANES)
    quarter = length // 4
    cos_b, sin_b = cosine(fine, length), cosine(fine - quarter, length)
    cos_a, sin_a = cosine(coarse, length), cosine(coarse - quarter, length)
    base_c = jnp.concatenate([cos_b, -sin_b], axis=0)
    base_s = jnp.concatenate([sin_b, cos_b], axis=0)
    turn_c = jnp.concatenate([cos_a, cos_a], axis=0)
    turn_s = jnp.concatenate([sin_a, sin_a], axis=0)
    full = length // LANES
    for a in range(pl.cdiv(length, LANES)):
        width = min(LANES, length - a * LANES)
        part = turn_c[:, a : a + 1] * base_c - turn_s[:, a : a + 1] * base_s
        high, low = split(part)
        waves8[0 : 2 * half, a * LANES : a * LANES + width] = high[:, :width]
        waves8[2 * half : 4 * half, a * LANES : a * LANES + width] = low[:, :width]

    for pair in range(slots // 2):
        both = jnp.concatenate([given_ref[2 * pair], given_ref[2 * pair + 1]], axis=1)
        coeffs[0:columns, pair * LANES : (pair + 1) * LANES] = both
        coeffs[columns : 2 * columns, pair * LANES : (pair + 1) * LANES] = both
    rest = coeffs.shape[1] - slots * KB
    coeffs[:, slots * KB :] = jnp.zeros((2 * columns, rest), bf16)

    field_copy.wait()
    cuts = list(range(0, full * LANES, WIDE)) + [full * LANES]
    cuts = [(b, min(b + WIDE, full * LANES)) for b in cuts[:-1]] + (
        [(full * LANES, length)] if full * LANES < length else []
    )
    total = jnp.zeros((4 * half, LANES), f32)
    for begin, end in cuts:
        high, low = split(field_buf[:, begin:end])
        part = waves8[:, begin:end]
        total = total + dot(part, high, ACROSS) + dot(part, low, ACROSS)
    fourier = total[: 2 * half] + total[2 * half :]

    lane = lax.broadcasted_iota(jnp.int32, (half, LANES), 1)
    pair_of = (lane // channels) % pair_dev
    weight = jnp.zeros((half, LANES), f32)
    for j in range(pair_dev):
        weight = jnp.where(pair_of == j, weight_ref[j], weight)
    weight = weight * (1.0 / length)

    def butterfly(value):
        turned = pltpu.roll(value, LANES // 2, 1)
        return (turned + jnp.where(lane < LANES // 2, value, -value)) * weight

    folded = [butterfly(fourier[:half]), butterfly(fourier[half:])]
    offsets = [r * spec_count * channels + spec * channels for r in range(2)]
    for pj in range(2 * pair_dev):
        placed = jnp.zeros((half, LANES), f32)
        for r in range(2):
            turned = pltpu.roll(
                folded[r], lax.rem(offsets[r] + (LANES - pj * channels), LANES), 1
            )
            here = (lane >= offsets[r]) & (lane < offsets[r] + channels)
            placed = jnp.where(here, turned, placed)
        stage[pl.ds(pj, half, stride=2 * pair_dev), :] = placed
    fold_send[...] = stage[...].astype(bf16)

    @pl.loop(1, dest_count)
    def _(t):
        fold_copy(place(t, dest_count, me), spec, lat).start()

    mine = pl.ds(pl.multiple_of(me * 16, 16), 16)
    fold_recv[spec, own, :] = fold_send[mine, :]

    m0, m1 = waves_ref[spec, 0, lat], waves_ref[spec, 1, lat]
    start1 = KB * ((L + KB - m0) >> SHIFT)
    lows, highs = [], []
    for b in range(lat_count):
        for s, (m, start) in enumerate(((m0, 0), (m1, start1))):
            lows.append(jnp.full((2 * pair_dev, LANES), start + KB * skip_ref[b, spec, s, lat]))
            highs.append(jnp.full((2 * pair_dev, LANES), L - m + start))
    lowest = jnp.concatenate(lows, axis=0)
    highest = jnp.concatenate(highs, axis=0)
    rows = lat_count * group
    row_q = lax.broadcasted_iota(jnp.int32, (rows, LANES), 0)
    lane_q = lax.broadcasted_iota(jnp.int32, (rows, LANES), 1)
    parity_ok = (lane_q & 1) == ((row_q // pair_dev) & 1)
    pick_row = lax.broadcasted_iota(jnp.int32, (rows, lat_count * 16), 0)
    pick_col = lax.broadcasted_iota(jnp.int32, (rows, lat_count * 16), 1)
    same_band = (pick_row // group) == (pick_col // 16)

    @pl.loop(1, lat_count)
    def _(t):
        table_copy(lat, place(t, lat_count, lat)).wait_recv()

    blocks = table_recv[...]
    for u in range(masked.shape[1] // WIDE):
        chosen = same_band & ((pick_col % 16) == u * pair_dev + pick_row % pair_dev)
        pick = jnp.where(chosen, 1.0, 0.0).astype(bf16)
        spread = dot(pick, blocks)
        for v in range(WIDE // LANES):
            at = u * WIDE + v * LANES
            spot = lane_q + at
            keep = parity_ok & (spot >= lowest) & (spot <= highest)
            piece = spread[:, v * LANES : (v + 1) * LANES]
            masked[:, at : at + LANES] = jnp.where(keep, piece, 0.0).astype(bf16)

    synthesis = dot(masked[...], coeffs[...], ACROSS)
    rounded = synthesis.astype(bf16).astype(f32)
    syn_send[...] = jnp.where(lane_q < columns, rounded, synthesis - rounded).astype(bf16)

    @pl.loop(1, dest_count)
    def _(t):
        syn_copy(place(t, dest_count, me), me).start()

    syn_recv[mine, :] = syn_send[own, :]

    @pl.loop(1, dest_count)
    def _(t):
        d = place(t, dest_count, me)
        fold_copy(me, d // lat_count, lax.rem(d, lat_count)).wait_recv()

    gathered = fold_recv[0].astype(f32)
    for q in range(1, spec_count):
        gathered = gathered + fold_recv[q].astype(f32)
    folded_own = gathered.T[:columns].astype(bf16)
    for u in range(masked.shape[1] // WIDE):
        part = dot(folded_own, masked[:, u * WIDE : (u + 1) * WIDE])
        for k in range(u * WIDE // KB, min((u + 1) * WIDE // KB, slots)):
            at = k * KB - u * WIDE
            spectrum_ref[k] = part[:, at : at + KB]

    @pl.loop(1, dest_count)
    def _(t):
        syn_copy(me, place(t, dest_count, me)).wait_recv()

    received = syn_recv[...].astype(f32)
    stage[...] = received + pltpu.roll(received, LANES // 2, 1)
    back = [jnp.zeros((half, LANES), f32) for _ in range(2)]
    for pj in range(2 * pair_dev):
        value = stage[pl.ds(pj, half, stride=2 * pair_dev), :]
        for r in range(2):
            turned = pltpu.roll(value, lax.rem(LANES + pj * channels - offsets[r], LANES), 1)
            back[r] = jnp.where((lane // channels) == pj, turned, back[r])
    back = jnp.concatenate([butterfly(back[0]), butterfly(back[1])], axis=0)
    high, low = split(jnp.concatenate([back, back], axis=0).T)
    for begin, end in cuts:
        part = waves8[:, begin:end]
        grid_ref[:, begin:end] = dot(high, part) + dot(low, part)

    @pl.loop(1, lat_count)
    def _(t):
        table_copy(place(t, lat_count, lat), lat).wait_send()

    @pl.loop(1, dest_count)
    def _(t):
        d = place(t, dest_count, me)
        fold_copy(d, spec, lat).wait_send()
        syn_copy(d, me).wait_send()


def on_device(
    lat_count, spec_count, field_grid, quad_weight, owner_waves, skip_blocks, legendre_table, given_spectrum
):
    hemispheres, pair_dev, channels, length = field_grid.shape
    slots = given_spectrum.shape[2]
    columns = 2 * given_spectrum.shape[4]
    dest_count = lat_count * spec_count
    rows = lat_count * 4 * pair_dev
    per_wide = WIDE // KB
    quarters = 16 // pair_dev
    table = legendre_table[0]
    table = jnp.pad(table, ((0, 0), (0, quarters * per_wide - slots), (0, 0), (0, 0)))
    table = table.reshape(lat_count, quarters, per_wide, pair_dev, KB)
    table = jnp.transpose(table, (0, 1, 3, 2, 4)).reshape(lat_count * 16, WIDE)
    half = 2 * dest_count
    f32, bf16 = jnp.float32, jnp.bfloat16
    vmem = pl.BlockSpec(memory_space=pltpu.VMEM)
    smem = pl.BlockSpec(memory_space=pltpu.SMEM)
    dma = pltpu.SemaphoreType.DMA
    spectrum, back_grid = pl.pallas_call(
        functools.partial(kernel, lat_count, spec_count),
        out_shape=(
            jax.ShapeDtypeStruct((slots, columns, KB), f32),
            jax.ShapeDtypeStruct((LANES, length), f32),
        ),
        in_specs=[smem, smem, smem, pl.BlockSpec(memory_space=pl.ANY), vmem, vmem],
        out_specs=(vmem, vmem),
        scratch_shapes=[
            pltpu.VMEM((LANES, length), f32),
            pltpu.VMEM((lat_count * 16, WIDE), bf16),
            pltpu.VMEM((dest_count * 16, LANES), f32),
            pltpu.VMEM((dest_count * 16, LANES), bf16),
            pltpu.VMEM((spec_count, rows, LANES), bf16),
            pltpu.VMEM((rows, LANES), bf16),
            pltpu.VMEM((dest_count * 16, LANES), bf16),
            pltpu.VMEM((4 * half, length), bf16),
            pltpu.VMEM((rows, quarters * WIDE), bf16),
            pltpu.VMEM((2 * columns, quarters * WIDE), bf16),
            dma,
            dma((lat_count,)),
            dma((lat_count,)),
            dma((dest_count,)),
            dma((dest_count,)),
            dma((dest_count,)),
            dma((dest_count,)),
        ],
        compiler_params=pltpu.CompilerParams(
            collective_id=0, has_side_effects=True, vmem_limit_bytes=48 * 2**20
        ),
        name="transform",
    )(
        jnp.transpose(owner_waves, (0, 2, 1)),
        jnp.transpose(skip_blocks, (0, 1, 3, 2)),
        quad_weight,
        field_grid.reshape(LANES, length),
        table,
        given_spectrum.reshape(slots, columns, KB),
    )
    return (spectrum.reshape(given_spectrum.shape), back_grid.reshape(field_grid.shape))


def solution(mesh):
    lat_count, spec_count = mesh.shape["lat"], mesh.shape["spec"]

    def body(*args):
        return on_device(lat_count, spec_count, *args)

    return jax.shard_map(
        body,
        mesh=mesh,
        in_specs=(
            P(None, "lat", ("group", "spec"), None),
            P("lat"),
            P(),
            P(),
            P("spec", None, None, "lat", None),
            P("spec", "lat", None, None, "group", None),
        ),
        out_specs=(
            P("spec", "lat", None, None, "group", None),
            P(None, "lat", ("group", "spec"), None),
        ),
        check_vma=False,
    )
```

```python
import functools
import math

import jax
import jax.numpy as jnp
from jax import lax
from jax.experimental import pallas as pl
from jax.experimental.pallas import tpu as pltpu
from jax.sharding import PartitionSpec as P

L = 1800
KB = 64
SHIFT = 6
LANES = 128
WIDE = 512
MESH = pl.DeviceIdType.MESH
ACROSS = (((1,), (1,)), ((), ()))
PLAIN = (((1,), (0,)), ((), ()))


def dot(a, b, dims=PLAIN):
    return lax.dot_general(a, b, dims, preferred_element_type=jnp.float32)


def cosine(phase, length):
    turns = jnp.floor(phase * (1.0 / length) + 0.5)
    angle = (phase - turns * length) * (2.0 * math.pi / length)
    z = angle * angle
    total = jnp.full_like(z, 1.0 / math.factorial(20))
    for n in range(18, -1, -2):
        sign = -1.0 if (n // 2) % 2 else 1.0
        total = total * z + sign / math.factorial(n)
    return total


def split(value):
    high = value.astype(jnp.bfloat16)
    return high, (value - high.astype(jnp.float32)).astype(jnp.bfloat16)


def kernel(
    lat_count,
    spec_count,
    waves_hbm,
    skip_hbm,
    weight_hbm,
    field_ref,
    table_ref,
    given_hbm,
    spectrum_ref,
    grid_ref,
    rest_ref,
    high_ref,
    low_ref,
    waves_ref,
    skip_ref,
    weight_ref,
    given_ref,
    field_buf,
    table_recv,
    stage,
    fold_send,
    fold_recv,
    syn_send,
    syn_recv,
    waves8,
    masked,
    coeffs,
    local_sem,
    table_send_sem,
    table_recv_sem,
    fold_send_sem,
    fold_recv_sem,
    syn_send_sem,
    syn_recv_sem,
):
    f32, bf16 = jnp.float32, jnp.bfloat16
    length = field_ref.shape[1]
    pair_dev = weight_ref.shape[0]
    channels = LANES // (2 * pair_dev)
    slots = given_ref.shape[0]
    columns = given_ref.shape[1]
    dest_count = lat_count * spec_count
    half = 2 * dest_count
    group = 4 * pair_dev
    lat = lax.axis_index("lat")
    spec = lax.axis_index("spec")
    me = spec * lat_count + lat

    def place(t, n, mine):
        return lax.rem(mine + t, n)

    def device(d):
        return {"spec": d // lat_count, "lat": lax.rem(d, lat_count)}

    waves_copy = pltpu.make_async_copy(waves_hbm, waves_ref, local_sem.at[0])
    skip_copy = pltpu.make_async_copy(skip_hbm, skip_ref, local_sem.at[1])
    weight_copy = pltpu.make_async_copy(weight_hbm, weight_ref, local_sem.at[2])
    given_copy = pltpu.make_async_copy(given_hbm, given_ref, local_sem.at[3])
    field_copy = pltpu.make_async_copy(field_ref, field_buf, local_sem.at[4])
    for copy in (waves_copy, skip_copy, weight_copy, given_copy, field_copy):
        copy.start()
    barrier = pltpu.get_barrier_semaphore()

    @pl.loop(1, dest_count)
    def _(t):
        pl.semaphore_signal(
            barrier, inc=1, device_id=device(place(t, dest_count, me)), device_id_type=MESH
        )

    pl.semaphore_wait(barrier, dest_count - 1)

    def table_copy(to, slot):
        return pltpu.make_async_remote_copy(
            src_ref=table_ref.at[pl.ds(to * 16, 16)],
            dst_ref=table_recv.at[pl.ds(slot * 16, 16)],
            send_sem=table_send_sem.at[to],
            recv_sem=table_recv_sem.at[slot],
            device_id={"lat": to},
            device_id_type=MESH,
        )

    def fold_copy(to, from_spec, from_lat):
        return pltpu.make_async_remote_copy(
            src_ref=fold_send.at[pl.ds(to * 16, 16)],
            dst_ref=fold_recv.at[from_spec, pl.ds(from_lat * 16, 16)],
            send_sem=fold_send_sem.at[to],
            recv_sem=fold_recv_sem.at[from_spec * lat_count + from_lat],
            device_id=device(to),
            device_id_type=MESH,
        )

    def syn_copy(to, slot):
        return pltpu.make_async_remote_copy(
            src_ref=syn_send.at[pl.ds(lax.rem(to, lat_count) * 16, 16)],
            dst_ref=syn_recv.at[pl.ds(slot * 16, 16)],
            send_sem=syn_send_sem.at[to],
            recv_sem=syn_recv_sem.at[slot],
            device_id=device(to),
            device_id_type=MESH,
        )

    @pl.loop(1, lat_count)
    def _(t):
        table_copy(place(t, lat_count, lat), lat).start()

    own = pl.ds(pl.multiple_of(lat * 16, 16), 16)
    mine = pl.ds(pl.multiple_of(me * 16, 16), 16)
    table_recv[own, :] = table_ref[own, :]

    for copy in (waves_copy, skip_copy, weight_copy):
        copy.wait()

    row8 = lax.broadcasted_iota(jnp.int32, (8, LANES), 0)
    tiles = []
    for tile in range(half // 8):
        wave = jnp.zeros((8, LANES), jnp.int32)
        for row in range(8):
            d, s = divmod(tile * 8 + row, 2)
            wave = jnp.where(row8 == row, waves_ref[d // lat_count, s, d % lat_count], wave)
        tiles.append(wave)
    wave = jnp.concatenate(tiles, axis=0).astype(f32)
    lane_half = lax.broadcasted_iota(jnp.int32, (half, LANES), 1).astype(f32)
    fine = wave * lane_half
    coarse = wave * (lane_half * LANES)
    quarter = length // 4
    cos_b, sin_b = cosine(fine, length), cosine(fine - quarter, length)
    cos_a, sin_a = cosine(coarse, length), cosine(coarse - quarter, length)
    base_c = jnp.concatenate([cos_b, -sin_b], axis=0)
    base_s = jnp.concatenate([sin_b, cos_b], axis=0)
    turn_c = jnp.concatenate([cos_a, cos_a], axis=0)
    turn_s = jnp.concatenate([sin_a, sin_a], axis=0)
    full = length // LANES
    for a in range(pl.cdiv(length, LANES)):
        width = min(LANES, length - a * LANES)
        part = turn_c[:, a : a + 1] * base_c - turn_s[:, a : a + 1] * base_s
        high, low = split(part)
        waves8[0 : 2 * half, a * LANES : a * LANES + width] = high[:, :width]
        waves8[2 * half : 4 * half, a * LANES : a * LANES + width] = low[:, :width]

    given_copy.wait()
    for pair in range(slots // 2):
        both = jnp.concatenate([given_ref[2 * pair], given_ref[2 * pair + 1]], axis=1)
        coeffs[0:columns, pair * LANES : (pair + 1) * LANES] = both
        coeffs[columns : 2 * columns, pair * LANES : (pair + 1) * LANES] = both
    rest = coeffs.shape[1] - slots * KB
    coeffs[:, slots * KB :] = jnp.zeros((2 * columns, rest), bf16)

    m0, m1 = waves_ref[spec, 0, lat], waves_ref[spec, 1, lat]
    start1 = KB * ((L + KB - m0) >> SHIFT)
    lows, highs = [], []
    for b in range(lat_count):
        for s, (m, start) in enumerate(((m0, 0), (m1, start1))):
            lows.append(jnp.full((2 * pair_dev, LANES), start + KB * skip_ref[b, spec, s, lat]))
            highs.append(jnp.full((2 * pair_dev, LANES), L - m + start))
    lowest = jnp.concatenate(lows, axis=0)
    highest = jnp.concatenate(highs, axis=0)
    rows = lat_count * group
    row_q = lax.broadcasted_iota(jnp.int32, (rows, LANES), 0)
    lane_q = lax.broadcasted_iota(jnp.int32, (rows, LANES), 1)
    parity_ok = (lane_q & 1) == ((row_q // pair_dev) & 1)
    pick_row = lax.broadcasted_iota(jnp.int32, (rows, lat_count * 16), 0)
    pick_col = lax.broadcasted_iota(jnp.int32, (rows, lat_count * 16), 1)
    same_band = (pick_row // group) == (pick_col // 16)

    @pl.loop(1, lat_count)
    def _(t):
        table_copy(lat, place(t, lat_count, lat)).wait_recv()

    blocks = table_recv[...]
    for u in range(masked.shape[1] // WIDE):
        chosen = same_band & ((pick_col % 16) == u * pair_dev + pick_row % pair_dev)
        pick = jnp.where(chosen, 1.0, 0.0).astype(bf16)
        spread = dot(pick, blocks)
        for v in range(WIDE // LANES):
            at = u * WIDE + v * LANES
            spot = lane_q + at
            keep = parity_ok & (spot >= lowest) & (spot <= highest)
            piece = spread[:, v * LANES : (v + 1) * LANES]
            masked[:, at : at + LANES] = jnp.where(keep, piece, 0.0).astype(bf16)

    synthesis = dot(masked[...], coeffs[...], ACROSS)
    rounded = synthesis.astype(bf16).astype(f32)
    syn_send[...] = jnp.where(lane_q < columns, rounded, synthesis - rounded).astype(bf16)

    @pl.loop(1, dest_count)
    def _(t):
        syn_copy(place(t, dest_count, me), me).start()

    syn_recv[mine, :] = syn_send[own, :]

    field_copy.wait()
    cuts = list(range(0, full * LANES, WIDE)) + [full * LANES]
    cuts = [(b, min(b + WIDE, full * LANES)) for b in cuts[:-1]] + (
        [(full * LANES, length)] if full * LANES < length else []
    )
    total = jnp.zeros((4 * half, LANES), f32)
    for begin, end in cuts:
        high, low = split(field_buf[:, begin:end])
        part = waves8[:, begin:end]
        total = total + dot(part, high, ACROSS) + dot(part, low, ACROSS)
    fourier = total[: 2 * half] + total[2 * half :]

    lane = lax.broadcasted_iota(jnp.int32, (half, LANES), 1)
    pair_of = (lane // channels) % pair_dev
    weight = jnp.zeros((half, LANES), f32)
    for j in range(pair_dev):
        weight = jnp.where(pair_of == j, weight_ref[j], weight)
    weight = weight * (1.0 / length)

    def butterfly(value):
        turned = pltpu.roll(value, LANES // 2, 1)
        return (turned + jnp.where(lane < LANES // 2, value, -value)) * weight

    folded = [butterfly(fourier[:half]), butterfly(fourier[half:])]
    offsets = [r * spec_count * channels + spec * channels for r in range(2)]
    for pj in range(2 * pair_dev):
        placed = jnp.zeros((half, LANES), f32)
        for r in range(2):
            turned = pltpu.roll(
                folded[r], lax.rem(offsets[r] + (LANES - pj * channels), LANES), 1
            )
            here = (lane >= offsets[r]) & (lane < offsets[r] + channels)
            placed = jnp.where(here, turned, placed)
        stage[pl.ds(pj, half, stride=2 * pair_dev), :] = placed
    fold_send[...] = stage[...].astype(bf16)

    @pl.loop(1, dest_count)
    def _(t):
        fold_copy(place(t, dest_count, me), spec, lat).start()

    fold_recv[spec, own, :] = fold_send[mine, :]

    @pl.loop(1, dest_count)
    def _(t):
        syn_copy(me, place(t, dest_count, me)).wait_recv()

    received = syn_recv[...].astype(f32)
    stage[...] = received + pltpu.roll(received, LANES // 2, 1)
    back = [jnp.zeros((half, LANES), f32) for _ in range(2)]
    for pj in range(2 * pair_dev):
        value = stage[pl.ds(pj, half, stride=2 * pair_dev), :]
        for r in range(2):
            turned = pltpu.roll(value, lax.rem(LANES + pj * channels - offsets[r], LANES), 1)
            back[r] = jnp.where((lane // channels) == pj, turned, back[r])
    back = jnp.concatenate([butterfly(back[0]), butterfly(back[1])], axis=0)
    high, low = split(jnp.concatenate([back, back], axis=0).T)
    high_ref[...] = high
    low_ref[...] = low
    done = grid_ref.shape[1]
    for begin, end in cuts:
        if end <= done:
            part = waves8[:, begin:end]
            grid_ref[:, begin:end] = dot(high, part) + dot(low, part)
    rest_ref[...] = waves8[:, done:]

    @pl.loop(1, dest_count)
    def _(t):
        d = place(t, dest_count, me)
        fold_copy(me, d // lat_count, lax.rem(d, lat_count)).wait_recv()

    gathered = fold_recv[0].astype(f32)
    for q in range(1, spec_count):
        gathered = gathered + fold_recv[q].astype(f32)
    folded_own = gathered.T[:columns].astype(bf16)
    for u in range(masked.shape[1] // WIDE):
        part = dot(folded_own, masked[:, u * WIDE : (u + 1) * WIDE])
        for k in range(u * WIDE // KB, min((u + 1) * WIDE // KB, slots)):
            at = k * KB - u * WIDE
            spectrum_ref[k] = part[:, at : at + KB]

    @pl.loop(1, lat_count)
    def _(t):
        table_copy(place(t, lat_count, lat), lat).wait_send()

    @pl.loop(1, dest_count)
    def _(t):
        d = place(t, dest_count, me)
        fold_copy(d, spec, lat).wait_send()
        syn_copy(d, me).wait_send()


def write_kernel(spectrum_in, grid_in, rest_ref, high_ref, low_ref, spectrum_ref, grid_ref, buf, sem):
    done = grid_in.shape[1]
    length = grid_ref.shape[1]
    copies = [
        pltpu.make_async_copy(grid_in, grid_ref.at[:, pl.ds(0, done)], sem.at[0]),
        pltpu.make_async_copy(spectrum_in, spectrum_ref, sem.at[1]),
    ]
    for copy in copies:
        copy.start()
    high, low = high_ref[...], low_ref[...]
    for n, begin in enumerate(range(0, length - done, WIDE)):
        end = min(begin + WIDE, length - done)
        if length - done - end < LANES:
            end = length - done
        if begin >= end or n >= sem.shape[0] - 2:
            break
        part = rest_ref[:, begin:end]
        buf[:, begin:end] = dot(high, part) + dot(low, part)
        copy = pltpu.make_async_copy(
            buf.at[:, pl.ds(begin, end - begin)],
            grid_ref.at[:, pl.ds(done + begin, end - begin)],
            sem.at[2 + n],
        )
        copy.start()
        copies.append(copy)
    for copy in copies:
        copy.wait()


def on_device(
    lat_count, spec_count, field_grid, quad_weight, owner_waves, skip_blocks, legendre_table, given_spectrum
):
    hemispheres, pair_dev, channels, length = field_grid.shape
    slots = given_spectrum.shape[2]
    columns = 2 * given_spectrum.shape[4]
    dest_count = lat_count * spec_count
    rows = lat_count * 4 * pair_dev
    per_wide = WIDE // KB
    quarters = 16 // pair_dev
    table = legendre_table[0]
    table = jnp.pad(table, ((0, 0), (0, quarters * per_wide - slots), (0, 0), (0, 0)))
    table = table.reshape(lat_count, quarters, per_wide, pair_dev, KB)
    table = jnp.transpose(table, (0, 1, 3, 2, 4)).reshape(lat_count * 16, WIDE)
    half = 2 * dest_count
    f32, bf16 = jnp.float32, jnp.bfloat16
    vmem = pl.BlockSpec(memory_space=pltpu.VMEM)
    smem = pl.BlockSpec(memory_space=pltpu.SMEM)
    dma = pltpu.SemaphoreType.DMA
    hbm = pl.BlockSpec(memory_space=pltpu.HBM)
    done = (length // 2) // WIDE * WIDE + WIDE
    rest = length - done
    parts = rest // WIDE + (1 if rest % WIDE >= LANES else 0)
    stack = jax.ShapeDtypeStruct((LANES, 4 * half), bf16)
    spectrum, first, waves_rest, high, low = pl.pallas_call(
        functools.partial(kernel, lat_count, spec_count),
        out_shape=(
            jax.ShapeDtypeStruct((slots, columns, KB), f32),
            jax.ShapeDtypeStruct((LANES, done), f32),
            jax.ShapeDtypeStruct((4 * half, rest), bf16),
            stack,
            stack,
        ),
        in_specs=[hbm, hbm, hbm, hbm, vmem, hbm],
        out_specs=(vmem,) * 5,
        scratch_shapes=[
            pltpu.SMEM((spec_count, 2, lat_count), jnp.int32),
            pltpu.SMEM((lat_count, spec_count, 2, lat_count), jnp.int32),
            pltpu.SMEM((pair_dev,), f32),
            pltpu.VMEM((slots, columns, KB), bf16),
            pltpu.VMEM((LANES, length), f32),
            pltpu.VMEM((lat_count * 16, WIDE), bf16),
            pltpu.VMEM((dest_count * 16, LANES), f32),
            pltpu.VMEM((dest_count * 16, LANES), bf16),
            pltpu.VMEM((spec_count, rows, LANES), bf16),
            pltpu.VMEM((rows, LANES), bf16),
            pltpu.VMEM((dest_count * 16, LANES), bf16),
            pltpu.VMEM((4 * half, length), bf16),
            pltpu.VMEM((rows, quarters * WIDE), bf16),
            pltpu.VMEM((2 * columns, quarters * WIDE), bf16),
            dma((5,)),
            dma((lat_count,)),
            dma((lat_count,)),
            dma((dest_count,)),
            dma((dest_count,)),
            dma((dest_count,)),
            dma((dest_count,)),
        ],
        compiler_params=pltpu.CompilerParams(
            collective_id=0, has_side_effects=True, vmem_limit_bytes=32 * 2**20
        ),
        name="transform",
    )(
        jnp.transpose(owner_waves, (0, 2, 1)),
        jnp.transpose(skip_blocks, (0, 1, 3, 2)),
        quad_weight,
        field_grid.reshape(LANES, length),
        table,
        given_spectrum.reshape(slots, columns, KB),
    )
    spectrum, back_grid = pl.pallas_call(
        write_kernel,
        out_shape=(
            jax.ShapeDtypeStruct((slots, columns, KB), f32),
            jax.ShapeDtypeStruct((LANES, length), f32),
        ),
        in_specs=[vmem] * 5,
        out_specs=(hbm, hbm),
        scratch_shapes=[pltpu.VMEM((LANES, rest), f32), dma((2 + parts,))],
        compiler_params=pltpu.CompilerParams(vmem_limit_bytes=16 * 2**20),
        name="write_out",
    )(spectrum, first, waves_rest, high, low)
    return (spectrum.reshape(given_spectrum.shape), back_grid.reshape(field_grid.shape))


def solution(mesh):
    lat_count, spec_count = mesh.shape["lat"], mesh.shape["spec"]

    def body(*args):
        return on_device(lat_count, spec_count, *args)

    return jax.shard_map(
        body,
        mesh=mesh,
        in_specs=(
            P(None, "lat", ("group", "spec"), None),
            P("lat"),
            P(),
            P(),
            P("spec", None, None, "lat", None),
            P("spec", "lat", None, None, "group", None),
        ),
        out_specs=(
            P("spec", "lat", None, None, "group", None),
            P(None, "lat", ("group", "spec"), None),
        ),
        check_vma=False,
    )
```

```python
import functools
import math

import jax
import jax.numpy as jnp
from jax import lax
from jax.experimental import pallas as pl
from jax.experimental.pallas import tpu as pltpu
from jax.sharding import PartitionSpec as P

L = 1800
KB = 64
SHIFT = 6
LANES = 128
WIDE = 512
MESH = pl.DeviceIdType.MESH
ACROSS = (((1,), (1,)), ((), ()))
PLAIN = (((1,), (0,)), ((), ()))


def dot(a, b, dims=PLAIN):
    return lax.dot_general(a, b, dims, preferred_element_type=jnp.float32)


def cosine(phase, length):
    turns = jnp.floor(phase * (1.0 / length) + 0.5)
    angle = (phase - turns * length) * (2.0 * math.pi / length)
    z = angle * angle
    total = jnp.full_like(z, 1.0 / math.factorial(20))
    for n in range(18, -1, -2):
        sign = -1.0 if (n // 2) % 2 else 1.0
        total = total * z + sign / math.factorial(n)
    return total


def split(value):
    high = value.astype(jnp.bfloat16)
    return high, (value - high.astype(jnp.float32)).astype(jnp.bfloat16)


def kernel(
    lat_count,
    spec_count,
    waves_hbm,
    skip_hbm,
    weight_hbm,
    field_ref,
    table_ref,
    given_hbm,
    spectrum_ref,
    grid_ref,
    rest_ref,
    high_ref,
    low_ref,
    waves_ref,
    skip_ref,
    weight_ref,
    given_ref,
    field_buf,
    table_recv,
    stage,
    fold_send,
    fold_recv,
    syn_send,
    syn_recv,
    waves8,
    masked,
    coeffs,
    local_sem,
    table_send_sem,
    table_recv_sem,
    fold_send_sem,
    fold_recv_sem,
    syn_send_sem,
    syn_recv_sem,
):
    f32, bf16 = jnp.float32, jnp.bfloat16
    length = field_ref.shape[1]
    pair_dev = weight_ref.shape[0]
    channels = LANES // (2 * pair_dev)
    slots = given_ref.shape[0]
    columns = given_ref.shape[1]
    dest_count = lat_count * spec_count
    half = 2 * dest_count
    group = 4 * pair_dev
    lat = lax.axis_index("lat")
    spec = lax.axis_index("spec")
    me = spec * lat_count + lat

    def place(t, n, mine):
        return lax.rem(mine + t, n)

    def device(d):
        return {"spec": d // lat_count, "lat": lax.rem(d, lat_count)}

    waves_copy = pltpu.make_async_copy(waves_hbm, waves_ref, local_sem.at[0])
    skip_copy = pltpu.make_async_copy(skip_hbm, skip_ref, local_sem.at[1])
    weight_copy = pltpu.make_async_copy(weight_hbm, weight_ref, local_sem.at[2])
    given_copy = pltpu.make_async_copy(given_hbm, given_ref, local_sem.at[3])
    field_copy = pltpu.make_async_copy(field_ref, field_buf, local_sem.at[4])
    for copy in (waves_copy, skip_copy, weight_copy, given_copy, field_copy):
        copy.start()
    barrier = pltpu.get_barrier_semaphore()

    @pl.loop(1, dest_count)
    def _(t):
        pl.semaphore_signal(
            barrier, inc=1, device_id=device(place(t, dest_count, me)), device_id_type=MESH
        )

    pl.semaphore_wait(barrier, dest_count - 1)

    def table_copy(to, slot):
        return pltpu.make_async_remote_copy(
            src_ref=table_ref.at[pl.ds(to * 16, 16)],
            dst_ref=table_recv.at[pl.ds(slot * 16, 16)],
            send_sem=table_send_sem.at[to],
            recv_sem=table_recv_sem.at[slot],
            device_id={"lat": to},
            device_id_type=MESH,
        )

    def fold_copy(to, from_spec, from_lat):
        return pltpu.make_async_remote_copy(
            src_ref=fold_send.at[pl.ds(to * 16, 16)],
            dst_ref=fold_recv.at[from_spec, pl.ds(from_lat * 16, 16)],
            send_sem=fold_send_sem.at[to],
            recv_sem=fold_recv_sem.at[from_spec * lat_count + from_lat],
            device_id=device(to),
            device_id_type=MESH,
        )

    def syn_copy(to, slot):
        return pltpu.make_async_remote_copy(
            src_ref=syn_send.at[pl.ds(lax.rem(to, lat_count) * 16, 16)],
            dst_ref=syn_recv.at[pl.ds(slot * 16, 16)],
            send_sem=syn_send_sem.at[to],
            recv_sem=syn_recv_sem.at[slot],
            device_id=device(to),
            device_id_type=MESH,
        )

    @pl.loop(1, lat_count)
    def _(t):
        table_copy(place(t, lat_count, lat), lat).start()

    own = pl.ds(pl.multiple_of(lat * 16, 16), 16)
    mine = pl.ds(pl.multiple_of(me * 16, 16), 16)
    table_recv[own, :] = table_ref[own, :]

    for copy in (waves_copy, skip_copy, weight_copy):
        copy.wait()

    row8 = lax.broadcasted_iota(jnp.int32, (8, LANES), 0)
    tiles = []
    for tile in range(half // 8):
        wave = jnp.zeros((8, LANES), jnp.int32)
        for row in range(8):
            d, s = divmod(tile * 8 + row, 2)
            wave = jnp.where(row8 == row, waves_ref[d // lat_count, s, d % lat_count], wave)
        tiles.append(wave)
    wave = jnp.concatenate(tiles, axis=0).astype(f32)
    lane_half = lax.broadcasted_iota(jnp.int32, (half, LANES), 1).astype(f32)
    fine = wave * lane_half
    coarse = wave * (lane_half * LANES)
    quarter = length // 4
    cos_b, sin_b = cosine(fine, length), cosine(fine - quarter, length)
    cos_a, sin_a = cosine(coarse, length), cosine(coarse - quarter, length)
    base_c = jnp.concatenate([cos_b, -sin_b], axis=0)
    base_s = jnp.concatenate([sin_b, cos_b], axis=0)
    turn_c = jnp.concatenate([cos_a, cos_a], axis=0)
    turn_s = jnp.concatenate([sin_a, sin_a], axis=0)
    full = length // LANES
    for a in range(pl.cdiv(length, LANES)):
        width = min(LANES, length - a * LANES)
        part = turn_c[:, a : a + 1] * base_c - turn_s[:, a : a + 1] * base_s
        high, low = split(part)
        waves8[0 : 2 * half, a * LANES : a * LANES + width] = high[:, :width]
        waves8[2 * half : 4 * half, a * LANES : a * LANES + width] = low[:, :width]

    given_copy.wait()
    for pair in range(slots // 2):
        both = jnp.concatenate([given_ref[2 * pair], given_ref[2 * pair + 1]], axis=1)
        coeffs[0:columns, pair * LANES : (pair + 1) * LANES] = both
        coeffs[columns : 2 * columns, pair * LANES : (pair + 1) * LANES] = both
    rest = coeffs.shape[1] - slots * KB
    coeffs[:, slots * KB :] = jnp.zeros((2 * columns, rest), bf16)

    m0, m1 = waves_ref[spec, 0, lat], waves_ref[spec, 1, lat]
    start1 = KB * ((L + KB - m0) >> SHIFT)
    lows, highs = [], []
    for b in range(lat_count):
        for s, (m, start) in enumerate(((m0, 0), (m1, start1))):
            lows.append(jnp.full((2 * pair_dev, LANES), start + KB * skip_ref[b, spec, s, lat]))
            highs.append(jnp.full((2 * pair_dev, LANES), L - m + start))
    lowest = jnp.concatenate(lows, axis=0)
    highest = jnp.concatenate(highs, axis=0)
    rows = lat_count * group
    row_q = lax.broadcasted_iota(jnp.int32, (rows, LANES), 0)
    lane_q = lax.broadcasted_iota(jnp.int32, (rows, LANES), 1)
    parity_ok = (lane_q & 1) == ((row_q // pair_dev) & 1)
    pick_row = lax.broadcasted_iota(jnp.int32, (rows, lat_count * 16), 0)
    pick_col = lax.broadcasted_iota(jnp.int32, (rows, lat_count * 16), 1)
    same_band = (pick_row // group) == (pick_col // 16)

    @pl.loop(1, lat_count)
    def _(t):
        table_copy(lat, place(t, lat_count, lat)).wait_recv()

    blocks = table_recv[...]
    for u in range(masked.shape[1] // WIDE):
        chosen = same_band & ((pick_col % 16) == u * pair_dev + pick_row % pair_dev)
        pick = jnp.where(chosen, 1.0, 0.0).astype(bf16)
        spread = dot(pick, blocks)
        for v in range(WIDE // LANES):
            at = u * WIDE + v * LANES
            spot = lane_q + at
            keep = parity_ok & (spot >= lowest) & (spot <= highest)
            piece = spread[:, v * LANES : (v + 1) * LANES]
            masked[:, at : at + LANES] = jnp.where(keep, piece, 0.0).astype(bf16)

    synthesis = dot(masked[...], coeffs[...], ACROSS)
    rounded = synthesis.astype(bf16).astype(f32)
    syn_send[...] = jnp.where(lane_q < columns, rounded, synthesis - rounded).astype(bf16)

    @pl.loop(1, dest_count)
    def _(t):
        syn_copy(place(t, dest_count, me), me).start()

    syn_recv[mine, :] = syn_send[own, :]

    field_copy.wait()
    cuts = list(range(0, full * LANES, WIDE)) + [full * LANES]
    cuts = [(b, min(b + WIDE, full * LANES)) for b in cuts[:-1]] + (
        [(full * LANES, length)] if full * LANES < length else []
    )
    total = jnp.zeros((4 * half, LANES), f32)
    for begin, end in cuts:
        high, low = split(field_buf[:, begin:end])
        part = waves8[:, begin:end]
        total = total + dot(part, high, ACROSS) + dot(part, low, ACROSS)
    fourier = total[: 2 * half] + total[2 * half :]

    lane = lax.broadcasted_iota(jnp.int32, (half, LANES), 1)
    pair_of = (lane // channels) % pair_dev
    weight = jnp.zeros((half, LANES), f32)
    for j in range(pair_dev):
        weight = jnp.where(pair_of == j, weight_ref[j], weight)
    weight = weight * (1.0 / length)

    def butterfly(value):
        turned = pltpu.roll(value, LANES // 2, 1)
        return (turned + jnp.where(lane < LANES // 2, value, -value)) * weight

    folded = [butterfly(fourier[:half]), butterfly(fourier[half:])]
    offsets = [r * spec_count * channels + spec * channels for r in range(2)]
    for pj in range(2 * pair_dev):
        placed = jnp.zeros((half, LANES), f32)
        for r in range(2):
            turned = pltpu.roll(
                folded[r], lax.rem(offsets[r] + (LANES - pj * channels), LANES), 1
            )
            here = (lane >= offsets[r]) & (lane < offsets[r] + channels)
            placed = jnp.where(here, turned, placed)
        stage[pl.ds(pj, half, stride=2 * pair_dev), :] = placed
    fold_send[...] = stage[...].astype(bf16)

    @pl.loop(1, dest_count)
    def _(t):
        fold_copy(place(t, dest_count, me), spec, lat).start()

    fold_recv[spec, own, :] = fold_send[mine, :]

    @pl.loop(1, dest_count)
    def _(t):
        syn_copy(me, place(t, dest_count, me)).wait_recv()

    received = syn_recv[...].astype(f32)
    stage[...] = received + pltpu.roll(received, LANES // 2, 1)
    back = [jnp.zeros((half, LANES), f32) for _ in range(2)]
    for pj in range(2 * pair_dev):
        value = stage[pl.ds(pj, half, stride=2 * pair_dev), :]
        for r in range(2):
            turned = pltpu.roll(value, lax.rem(LANES + pj * channels - offsets[r], LANES), 1)
            back[r] = jnp.where((lane // channels) == pj, turned, back[r])
    back = jnp.concatenate([butterfly(back[0]), butterfly(back[1])], axis=0)
    high, low = split(jnp.concatenate([back, back], axis=0).T)
    high_ref[...] = high
    low_ref[...] = low
    done = grid_ref.shape[1]
    for begin, end in cuts:
        if end <= done:
            part = waves8[:, begin:end]
            grid_ref[:, begin:end] = dot(high, part) + dot(low, part)
    rest_ref[...] = waves8[:, done:]

    @pl.loop(1, dest_count)
    def _(t):
        d = place(t, dest_count, me)
        fold_copy(me, d // lat_count, lax.rem(d, lat_count)).wait_recv()

    gathered = fold_recv[0].astype(f32)
    for q in range(1, spec_count):
        gathered = gathered + fold_recv[q].astype(f32)
    folded_own = gathered.T[:columns].astype(bf16)
    for u in range(masked.shape[1] // WIDE):
        part = dot(folded_own, masked[:, u * WIDE : (u + 1) * WIDE])
        for k in range(u * WIDE // KB, min((u + 1) * WIDE // KB, slots)):
            at = k * KB - u * WIDE
            spectrum_ref[k] = part[:, at : at + KB]

    @pl.loop(1, lat_count)
    def _(t):
        table_copy(place(t, lat_count, lat), lat).wait_send()

    @pl.loop(1, dest_count)
    def _(t):
        d = place(t, dest_count, me)
        fold_copy(d, spec, lat).wait_send()
        syn_copy(d, me).wait_send()


def stay(array):
    return pltpu.with_memory_space_constraint(array, pltpu.HBM)


def write_kernel(spectrum_in, grid_in, rest_ref, high_ref, low_ref, spectrum_ref, grid_ref, buf, sem):
    done = grid_in.shape[1]
    length = grid_ref.shape[1]
    copies = [
        pltpu.make_async_copy(grid_in, grid_ref.at[:, pl.ds(0, done)], sem.at[0]),
        pltpu.make_async_copy(spectrum_in, spectrum_ref, sem.at[1]),
    ]
    for copy in copies:
        copy.start()
    high, low = high_ref[...], low_ref[...]
    for n, begin in enumerate(range(0, length - done, WIDE)):
        end = min(begin + WIDE, length - done)
        if length - done - end < LANES:
            end = length - done
        if begin >= end or n >= sem.shape[0] - 2:
            break
        part = rest_ref[:, begin:end]
        buf[:, begin:end] = dot(high, part) + dot(low, part)
        copy = pltpu.make_async_copy(
            buf.at[:, pl.ds(begin, end - begin)],
            grid_ref.at[:, pl.ds(done + begin, end - begin)],
            sem.at[2 + n],
        )
        copy.start()
        copies.append(copy)
    for copy in copies:
        copy.wait()


def on_device(
    lat_count, spec_count, field_grid, quad_weight, owner_waves, skip_blocks, legendre_table, given_spectrum
):
    hemispheres, pair_dev, channels, length = field_grid.shape
    slots = given_spectrum.shape[2]
    columns = 2 * given_spectrum.shape[4]
    dest_count = lat_count * spec_count
    rows = lat_count * 4 * pair_dev
    per_wide = WIDE // KB
    quarters = 16 // pair_dev
    table = legendre_table[0]
    table = jnp.pad(table, ((0, 0), (0, quarters * per_wide - slots), (0, 0), (0, 0)))
    table = table.reshape(lat_count, quarters, per_wide, pair_dev, KB)
    table = jnp.transpose(table, (0, 1, 3, 2, 4)).reshape(lat_count * 16, WIDE)
    half = 2 * dest_count
    f32, bf16 = jnp.float32, jnp.bfloat16
    vmem = pl.BlockSpec(memory_space=pltpu.VMEM)
    smem = pl.BlockSpec(memory_space=pltpu.SMEM)
    dma = pltpu.SemaphoreType.DMA
    hbm = pl.BlockSpec(memory_space=pltpu.HBM)
    done = (length // 2) // WIDE * WIDE + WIDE
    rest = length - done
    parts = rest // WIDE + (1 if rest % WIDE >= LANES else 0)
    stack = jax.ShapeDtypeStruct((LANES, 4 * half), bf16)
    spectrum, first, waves_rest, high, low = pl.pallas_call(
        functools.partial(kernel, lat_count, spec_count),
        out_shape=(
            jax.ShapeDtypeStruct((slots, columns, KB), f32),
            jax.ShapeDtypeStruct((LANES, done), f32),
            jax.ShapeDtypeStruct((4 * half, rest), bf16),
            stack,
            stack,
        ),
        in_specs=[hbm, hbm, hbm, hbm, vmem, hbm],
        out_specs=(vmem,) * 5,
        scratch_shapes=[
            pltpu.SMEM((spec_count, 2, lat_count), jnp.int32),
            pltpu.SMEM((lat_count, spec_count, 2, lat_count), jnp.int32),
            pltpu.SMEM((pair_dev,), f32),
            pltpu.VMEM((slots, columns, KB), bf16),
            pltpu.VMEM((LANES, length), f32),
            pltpu.VMEM((lat_count * 16, WIDE), bf16),
            pltpu.VMEM((dest_count * 16, LANES), f32),
            pltpu.VMEM((dest_count * 16, LANES), bf16),
            pltpu.VMEM((spec_count, rows, LANES), bf16),
            pltpu.VMEM((rows, LANES), bf16),
            pltpu.VMEM((dest_count * 16, LANES), bf16),
            pltpu.VMEM((4 * half, length), bf16),
            pltpu.VMEM((rows, quarters * WIDE), bf16),
            pltpu.VMEM((2 * columns, quarters * WIDE), bf16),
            dma((5,)),
            dma((lat_count,)),
            dma((lat_count,)),
            dma((dest_count,)),
            dma((dest_count,)),
            dma((dest_count,)),
            dma((dest_count,)),
        ],
        compiler_params=pltpu.CompilerParams(
            collective_id=0, has_side_effects=True, vmem_limit_bytes=32 * 2**20
        ),
        name="transform",
    )(
        stay(jnp.transpose(owner_waves, (0, 2, 1))),
        stay(jnp.transpose(skip_blocks, (0, 1, 3, 2))),
        stay(quad_weight),
        stay(field_grid.reshape(LANES, length)),
        table,
        stay(given_spectrum.reshape(slots, columns, KB)),
    )
    spectrum, back_grid = pl.pallas_call(
        write_kernel,
        out_shape=(
            jax.ShapeDtypeStruct((slots, columns, KB), f32),
            jax.ShapeDtypeStruct((LANES, length), f32),
        ),
        in_specs=[vmem] * 5,
        out_specs=(hbm, hbm),
        scratch_shapes=[pltpu.VMEM((LANES, rest), f32), dma((2 + parts,))],
        compiler_params=pltpu.CompilerParams(vmem_limit_bytes=16 * 2**20),
        name="write_out",
    )(spectrum, first, waves_rest, high, low)
    return (spectrum.reshape(given_spectrum.shape), back_grid.reshape(field_grid.shape))


def solution(mesh):
    lat_count, spec_count = mesh.shape["lat"], mesh.shape["spec"]

    def body(*args):
        return on_device(lat_count, spec_count, *args)

    return jax.shard_map(
        body,
        mesh=mesh,
        in_specs=(
            P(None, "lat", ("group", "spec"), None),
            P("lat"),
            P(),
            P(),
            P("spec", None, None, "lat", None),
            P("spec", "lat", None, None, "group", None),
        ),
        out_specs=(
            P("spec", "lat", None, None, "group", None),
            P(None, "lat", ("group", "spec"), None),
        ),
        check_vma=False,
    )
```

```python
import functools
import math

import jax
import jax.numpy as jnp
from jax import lax
from jax.experimental import pallas as pl
from jax.experimental.pallas import tpu as pltpu
from jax.sharding import PartitionSpec as P

L = 1800
KB = 64
SHIFT = 6
LANES = 128
WIDE = 512
MESH = pl.DeviceIdType.MESH
ACROSS = (((1,), (1,)), ((), ()))
PLAIN = (((1,), (0,)), ((), ()))


def dot(a, b, dims=PLAIN):
    return lax.dot_general(a, b, dims, preferred_element_type=jnp.float32)


def cosine(phase, length):
    turns = jnp.floor(phase * (1.0 / length) + 0.5)
    angle = (phase - turns * length) * (2.0 * math.pi / length)
    z = angle * angle
    total = jnp.full_like(z, 1.0 / math.factorial(20))
    for n in range(18, -1, -2):
        sign = -1.0 if (n // 2) % 2 else 1.0
        total = total * z + sign / math.factorial(n)
    return total


def split(value):
    high = value.astype(jnp.bfloat16)
    return high, (value - high.astype(jnp.float32)).astype(jnp.bfloat16)


def kernel(
    lat_count,
    spec_count,
    waves_hbm,
    skip_hbm,
    weight_hbm,
    field_ref,
    table_hbm,
    given_hbm,
    spectrum_ref,
    grid_ref,
    rest_ref,
    high_ref,
    low_ref,
    waves_ref,
    skip_ref,
    weight_ref,
    given_ref,
    table_raw,
    table_stage,
    table_ref,
    field_buf,
    table_recv,
    stage,
    fold_send,
    fold_recv,
    syn_send,
    syn_recv,
    waves8,
    masked,
    coeffs,
    local_sem,
    table_send_sem,
    table_recv_sem,
    fold_send_sem,
    fold_recv_sem,
    syn_send_sem,
    syn_recv_sem,
):
    f32, bf16 = jnp.float32, jnp.bfloat16
    length = field_ref.shape[1]
    pair_dev = weight_ref.shape[0]
    channels = LANES // (2 * pair_dev)
    slots = given_ref.shape[0]
    columns = given_ref.shape[1]
    dest_count = lat_count * spec_count
    half = 2 * dest_count
    group = 4 * pair_dev
    lat = lax.axis_index("lat")
    spec = lax.axis_index("spec")
    me = spec * lat_count + lat

    lats = [lat] + [lax.rem(lat + t, lat_count) for t in range(1, lat_count)]
    specs = [spec] + [lax.rem(spec + t, spec_count) for t in range(1, spec_count)]
    others = [(q, b) for b in lats for q in specs][1:]

    def finish(buf, blocks, sem):
        part = buf.at[pl.ds(0, blocks * 16)]
        pltpu.make_async_copy(part, part, sem).wait()

    waves_copy = pltpu.make_async_copy(waves_hbm, waves_ref, local_sem.at[0])
    skip_copy = pltpu.make_async_copy(skip_hbm, skip_ref, local_sem.at[1])
    weight_copy = pltpu.make_async_copy(weight_hbm, weight_ref, local_sem.at[2])
    given_copy = pltpu.make_async_copy(given_hbm, given_ref, local_sem.at[3])
    field_copy = pltpu.make_async_copy(field_ref, field_buf, local_sem.at[4])
    table_move = pltpu.make_async_copy(table_hbm, table_raw, local_sem.at[5])
    table_move.start()
    barrier = pltpu.get_barrier_semaphore()
    for q, b in others:
        pl.semaphore_signal(
            barrier, inc=1, device_id={"spec": q, "lat": b}, device_id_type=MESH
        )
    for copy in (waves_copy, skip_copy, weight_copy, given_copy, field_copy):
        copy.start()

    table_move.wait()
    per_row = WIDE // LANES

    @pl.loop(0, lat_count)
    def _(o):
        for t in range(table_ref.shape[1] * 16 // (pair_dev * LANES)):
            u, v = t // per_row, t % per_row
            if 2 * t < slots:
                both = jnp.concatenate(
                    [table_raw[o, 2 * t].astype(f32), table_raw[o, 2 * t + 1].astype(f32)], axis=1
                )
            else:
                both = jnp.zeros((pair_dev, LANES), f32)
            table_stage[o, u * pair_dev : (u + 1) * pair_dev, v * LANES : (v + 1) * LANES] = both

    table_ref[...] = table_stage[...].reshape(table_ref.shape).astype(bf16)
    pl.semaphore_wait(barrier, dest_count - 1)
    for b in lats[1:]:
        pltpu.make_async_remote_copy(
            src_ref=table_ref.at[pl.ds(b * 16, 16)],
            dst_ref=table_recv.at[pl.ds(lat * 16, 16)],
            send_sem=table_send_sem,
            recv_sem=table_recv_sem,
            device_id={"lat": b},
            device_id_type=MESH,
        ).start()

    own = pl.ds(pl.multiple_of(lat * 16, 16), 16)
    mine = pl.ds(pl.multiple_of(me * 16, 16), 16)
    table_recv[own, :] = table_ref[own, :]
    for copy in (waves_copy, skip_copy, weight_copy):
        copy.wait()

    row8 = lax.broadcasted_iota(jnp.int32, (8, LANES), 0)
    tiles = []
    for tile in range(half // 8):
        wave = jnp.zeros((8, LANES), jnp.int32)
        for row in range(8):
            d, s = divmod(tile * 8 + row, 2)
            wave = jnp.where(row8 == row, waves_ref[d // lat_count, s, d % lat_count], wave)
        tiles.append(wave)
    wave = jnp.concatenate(tiles, axis=0).astype(f32)
    lane_half = lax.broadcasted_iota(jnp.int32, (half, LANES), 1).astype(f32)
    fine = wave * lane_half
    coarse = wave * (lane_half * LANES)
    quarter = length // 4
    cos_b, sin_b = cosine(fine, length), cosine(fine - quarter, length)
    cos_a, sin_a = cosine(coarse, length), cosine(coarse - quarter, length)
    base_c = jnp.concatenate([cos_b, -sin_b], axis=0)
    base_s = jnp.concatenate([sin_b, cos_b], axis=0)
    turn_c = jnp.concatenate([cos_a, cos_a], axis=0)
    turn_s = jnp.concatenate([sin_a, sin_a], axis=0)
    full = length // LANES
    for a in range(pl.cdiv(length, LANES)):
        width = min(LANES, length - a * LANES)
        part = turn_c[:, a : a + 1] * base_c - turn_s[:, a : a + 1] * base_s
        high, low = split(part)
        waves8[0 : 2 * half, a * LANES : a * LANES + width] = high[:, :width]
        waves8[2 * half : 4 * half, a * LANES : a * LANES + width] = low[:, :width]

    given_copy.wait()
    for pair in range(slots // 2):
        both = jnp.concatenate([given_ref[2 * pair], given_ref[2 * pair + 1]], axis=1)
        coeffs[0:columns, pair * LANES : (pair + 1) * LANES] = both
        coeffs[columns : 2 * columns, pair * LANES : (pair + 1) * LANES] = both
    rest = coeffs.shape[1] - slots * KB
    coeffs[:, slots * KB :] = jnp.zeros((2 * columns, rest), bf16)

    field_copy.wait()
    cuts = list(range(0, full * LANES, WIDE)) + [full * LANES]
    cuts = [(b, min(b + WIDE, full * LANES)) for b in cuts[:-1]] + (
        [(full * LANES, length)] if full * LANES < length else []
    )
    total = jnp.zeros((4 * half, LANES), f32)
    for begin, end in cuts:
        high, low = split(field_buf[:, begin:end])
        part = waves8[:, begin:end]
        total = total + dot(part, high, ACROSS) + dot(part, low, ACROSS)
    fourier = total[: 2 * half] + total[2 * half :]

    lane = lax.broadcasted_iota(jnp.int32, (half, LANES), 1)
    pair_of = (lane // channels) % pair_dev
    weight = jnp.zeros((half, LANES), f32)
    for j in range(pair_dev):
        weight = jnp.where(pair_of == j, weight_ref[j], weight)
    weight = weight * (1.0 / length)

    def butterfly(value):
        turned = pltpu.roll(value, LANES // 2, 1)
        return (turned + jnp.where(lane < LANES // 2, value, -value)) * weight

    folded = [butterfly(fourier[:half]), butterfly(fourier[half:])]
    offsets = [r * spec_count * channels + spec * channels for r in range(2)]
    for pj in range(2 * pair_dev):
        placed = jnp.zeros((half, LANES), f32)
        for r in range(2):
            turned = pltpu.roll(
                folded[r], lax.rem(offsets[r] + (LANES - pj * channels), LANES), 1
            )
            here = (lane >= offsets[r]) & (lane < offsets[r] + channels)
            placed = jnp.where(here, turned, placed)
        stage[pl.ds(pj, half, stride=2 * pair_dev), :] = placed
    fold_send[...] = stage[...].astype(bf16)

    for q, b in others:
        pltpu.make_async_remote_copy(
            src_ref=fold_send.at[pl.ds((q * lat_count + b) * 16, 16)],
            dst_ref=fold_recv.at[pl.ds(me * 16, 16)],
            send_sem=fold_send_sem,
            recv_sem=fold_recv_sem,
            device_id={"spec": q, "lat": b},
            device_id_type=MESH,
        ).start()

    fold_recv[mine, :] = fold_send[mine, :]

    m0, m1 = waves_ref[spec, 0, lat], waves_ref[spec, 1, lat]
    start1 = KB * ((L + KB - m0) >> SHIFT)
    lows, highs = [], []
    for b in range(lat_count):
        for s, (m, start) in enumerate(((m0, 0), (m1, start1))):
            lows.append(jnp.full((2 * pair_dev, LANES), start + KB * skip_ref[b, spec, s, lat]))
            highs.append(jnp.full((2 * pair_dev, LANES), L - m + start))
    lowest = jnp.concatenate(lows, axis=0)
    highest = jnp.concatenate(highs, axis=0)
    rows = lat_count * group
    row_q = lax.broadcasted_iota(jnp.int32, (rows, LANES), 0)
    lane_q = lax.broadcasted_iota(jnp.int32, (rows, LANES), 1)
    parity_ok = (lane_q & 1) == ((row_q // pair_dev) & 1)
    pick_row = lax.broadcasted_iota(jnp.int32, (rows, lat_count * 16), 0)
    pick_col = lax.broadcasted_iota(jnp.int32, (rows, lat_count * 16), 1)
    same_band = (pick_row // group) == (pick_col // 16)

    finish(table_recv, lat_count - 1, table_recv_sem)

    blocks = table_recv[...]
    for u in range(masked.shape[1] // WIDE):
        chosen = same_band & ((pick_col % 16) == u * pair_dev + pick_row % pair_dev)
        pick = jnp.where(chosen, 1.0, 0.0).astype(bf16)
        spread = dot(pick, blocks)
        for v in range(WIDE // LANES):
            at = u * WIDE + v * LANES
            spot = lane_q + at
            keep = parity_ok & (spot >= lowest) & (spot <= highest)
            piece = spread[:, v * LANES : (v + 1) * LANES]
            masked[:, at : at + LANES] = jnp.where(keep, piece, 0.0).astype(bf16)

    synthesis = dot(masked[...], coeffs[...], ACROSS)
    rounded = synthesis.astype(bf16).astype(f32)
    syn_send[...] = jnp.where(lane_q < columns, rounded, synthesis - rounded).astype(bf16)

    for q, b in others:
        pltpu.make_async_remote_copy(
            src_ref=syn_send.at[pl.ds(b * 16, 16)],
            dst_ref=syn_recv.at[pl.ds(me * 16, 16)],
            send_sem=syn_send_sem,
            recv_sem=syn_recv_sem,
            device_id={"spec": q, "lat": b},
            device_id_type=MESH,
        ).start()

    syn_recv[mine, :] = syn_send[own, :]

    finish(fold_recv, dest_count - 1, fold_recv_sem)
    gathered = fold_recv[0:rows, :].astype(f32)
    for q in range(1, spec_count):
        gathered = gathered + fold_recv[q * rows : (q + 1) * rows, :].astype(f32)
    folded_own = gathered.T[:columns].astype(bf16)
    for u in range(masked.shape[1] // WIDE):
        part = dot(folded_own, masked[:, u * WIDE : (u + 1) * WIDE])
        for k in range(u * WIDE // KB, min((u + 1) * WIDE // KB, slots)):
            at = k * KB - u * WIDE
            spectrum_ref[k] = part[:, at : at + KB]

    finish(syn_recv, dest_count - 1, syn_recv_sem)

    received = syn_recv[...].astype(f32)
    stage[...] = received + pltpu.roll(received, LANES // 2, 1)
    back = [jnp.zeros((half, LANES), f32) for _ in range(2)]
    for pj in range(2 * pair_dev):
        value = stage[pl.ds(pj, half, stride=2 * pair_dev), :]
        for r in range(2):
            turned = pltpu.roll(value, lax.rem(LANES + pj * channels - offsets[r], LANES), 1)
            back[r] = jnp.where((lane // channels) == pj, turned, back[r])
    back = jnp.concatenate([butterfly(back[0]), butterfly(back[1])], axis=0)
    high, low = split(jnp.concatenate([back, back], axis=0).T)
    high_ref[...] = high
    low_ref[...] = low
    done = grid_ref.shape[1]
    for begin, end in cuts:
        if end <= done:
            part = waves8[:, begin:end]
            grid_ref[:, begin:end] = dot(high, part) + dot(low, part)
    rest_ref[...] = waves8[:, done:]

    finish(table_recv, lat_count - 1, table_send_sem)
    finish(fold_recv, dest_count - 1, fold_send_sem)
    finish(syn_recv, dest_count - 1, syn_send_sem)


def stay(array):
    return pltpu.with_memory_space_constraint(array, pltpu.HBM)


def write_kernel(spectrum_in, grid_in, rest_ref, high_ref, low_ref, spectrum_ref, grid_ref, buf, sem):
    done = grid_in.shape[1]
    length = grid_ref.shape[1]
    copies = [
        pltpu.make_async_copy(grid_in, grid_ref.at[:, pl.ds(0, done)], sem.at[0]),
        pltpu.make_async_copy(spectrum_in, spectrum_ref, sem.at[1]),
    ]
    for copy in copies:
        copy.start()
    high, low = high_ref[...], low_ref[...]
    for n, begin in enumerate(range(0, length - done, WIDE)):
        end = min(begin + WIDE, length - done)
        if length - done - end < LANES:
            end = length - done
        if begin >= end or n >= sem.shape[0] - 2:
            break
        part = rest_ref[:, begin:end]
        buf[:, begin:end] = dot(high, part) + dot(low, part)
        copy = pltpu.make_async_copy(
            buf.at[:, pl.ds(begin, end - begin)],
            grid_ref.at[:, pl.ds(done + begin, end - begin)],
            sem.at[2 + n],
        )
        copy.start()
        copies.append(copy)
    for copy in copies:
        copy.wait()


def on_device(
    lat_count, spec_count, field_grid, quad_weight, owner_waves, skip_blocks, legendre_table, given_spectrum
):
    hemispheres, pair_dev, channels, length = field_grid.shape
    slots = given_spectrum.shape[2]
    columns = 2 * given_spectrum.shape[4]
    dest_count = lat_count * spec_count
    rows = lat_count * 4 * pair_dev
    quarters = 16 // pair_dev
    half = 2 * dest_count
    f32, bf16 = jnp.float32, jnp.bfloat16
    vmem = pl.BlockSpec(memory_space=pltpu.VMEM)
    dma = pltpu.SemaphoreType.DMA
    hbm = pl.BlockSpec(memory_space=pltpu.HBM)
    done = (length // 2) // WIDE * WIDE + WIDE
    rest = length - done
    parts = rest // WIDE + (1 if rest % WIDE >= LANES else 0)
    stack = jax.ShapeDtypeStruct((LANES, 4 * half), bf16)
    spectrum, first, waves_rest, high, low = pl.pallas_call(
        functools.partial(kernel, lat_count, spec_count),
        out_shape=(
            jax.ShapeDtypeStruct((slots, columns, KB), f32),
            jax.ShapeDtypeStruct((LANES, done), f32),
            jax.ShapeDtypeStruct((4 * half, rest), bf16),
            stack,
            stack,
        ),
        in_specs=[hbm] * 6,
        out_specs=(vmem,) * 5,
        scratch_shapes=[
            pltpu.SMEM((spec_count, 2, lat_count), jnp.int32),
            pltpu.SMEM((lat_count, spec_count, 2, lat_count), jnp.int32),
            pltpu.SMEM((pair_dev,), f32),
            pltpu.VMEM((slots, columns, KB), bf16),
            pltpu.VMEM((lat_count, slots, pair_dev, KB), bf16),
            pltpu.VMEM((lat_count, 16, WIDE), f32),
            pltpu.VMEM((lat_count * 16, WIDE), bf16),
            pltpu.VMEM((LANES, length), f32),
            pltpu.VMEM((lat_count * 16, WIDE), bf16),
            pltpu.VMEM((dest_count * 16, LANES), f32),
            pltpu.VMEM((dest_count * 16, LANES), bf16),
            pltpu.VMEM((spec_count * rows, LANES), bf16),
            pltpu.VMEM((rows, LANES), bf16),
            pltpu.VMEM((dest_count * 16, LANES), bf16),
            pltpu.VMEM((4 * half, length), bf16),
            pltpu.VMEM((rows, quarters * WIDE), bf16),
            pltpu.VMEM((2 * columns, quarters * WIDE), bf16),
            dma((6,)),
            dma,
            dma,
            dma,
            dma,
            dma,
            dma,
        ],
        compiler_params=pltpu.CompilerParams(
            collective_id=0, has_side_effects=True, vmem_limit_bytes=32 * 2**20
        ),
        name="transform",
    )(
        stay(jnp.transpose(owner_waves, (0, 2, 1))),
        stay(jnp.transpose(skip_blocks, (0, 1, 3, 2))),
        stay(quad_weight),
        stay(field_grid.reshape(LANES, length)),
        stay(legendre_table[0]),
        stay(given_spectrum.reshape(slots, columns, KB)),
    )
    spectrum, back_grid = pl.pallas_call(
        write_kernel,
        out_shape=(
            jax.ShapeDtypeStruct((slots, columns, KB), f32),
            jax.ShapeDtypeStruct((LANES, length), f32),
        ),
        in_specs=[vmem] * 5,
        out_specs=(hbm, hbm),
        scratch_shapes=[pltpu.VMEM((LANES, rest), f32), dma((2 + parts,))],
        compiler_params=pltpu.CompilerParams(vmem_limit_bytes=16 * 2**20),
        name="write_out",
    )(spectrum, first, waves_rest, high, low)
    return (spectrum.reshape(given_spectrum.shape), back_grid.reshape(field_grid.shape))


def solution(mesh):
    lat_count, spec_count = mesh.shape["lat"], mesh.shape["spec"]

    def body(*args):
        return on_device(lat_count, spec_count, *args)

    return jax.shard_map(
        body,
        mesh=mesh,
        in_specs=(
            P(None, "lat", ("group", "spec"), None),
            P("lat"),
            P(),
            P(),
            P("spec", None, None, "lat", None),
            P("spec", "lat", None, None, "group", None),
        ),
        out_specs=(
            P("spec", "lat", None, None, "group", None),
            P(None, "lat", ("group", "spec"), None),
        ),
        check_vma=False,
    )
```

```python
import functools
import math

import jax
import jax.numpy as jnp
from jax import lax
from jax.experimental import pallas as pl
from jax.experimental.pallas import tpu as pltpu
from jax.sharding import PartitionSpec as P

L = 1800
KB = 64
SHIFT = 6
LANES = 128
WIDE = 512
MESH = pl.DeviceIdType.MESH
ACROSS = (((1,), (1,)), ((), ()))
PLAIN = (((1,), (0,)), ((), ()))


def dot(a, b, dims=PLAIN):
    return lax.dot_general(a, b, dims, preferred_element_type=jnp.float32)


def cosine(phase, length):
    turns = jnp.floor(phase * (1.0 / length) + 0.5)
    angle = (phase - turns * length) * (2.0 * math.pi / length)
    z = angle * angle
    total = jnp.full_like(z, 1.0 / math.factorial(20))
    for n in range(18, -1, -2):
        sign = -1.0 if (n // 2) % 2 else 1.0
        total = total * z + sign / math.factorial(n)
    return total


def split(value):
    high = value.astype(jnp.bfloat16)
    return high, (value - high.astype(jnp.float32)).astype(jnp.bfloat16)


def kernel(
    lat_count,
    spec_count,
    waves_hbm,
    skip_hbm,
    weight_hbm,
    field_ref,
    table_hbm,
    given_hbm,
    spectrum_ref,
    waves8,
    back_ref,
    waves_ref,
    skip_ref,
    weight_ref,
    given_ref,
    table_raw,
    table_stage,
    table_ref,
    field_buf,
    table_recv,
    stage,
    fold_send,
    fold_recv,
    syn_send,
    syn_recv,
    masked,
    coeffs,
    local_sem,
    table_send_sem,
    table_recv_sem,
    fold_send_sem,
    fold_recv_sem,
    syn_send_sem,
    syn_recv_sem,
):
    f32, bf16 = jnp.float32, jnp.bfloat16
    length = field_ref.shape[1]
    pair_dev = weight_ref.shape[0]
    channels = LANES // (2 * pair_dev)
    slots = given_ref.shape[0]
    columns = given_ref.shape[1]
    dest_count = lat_count * spec_count
    half = 2 * dest_count
    group = 4 * pair_dev
    lat = lax.axis_index("lat")
    spec = lax.axis_index("spec")
    me = spec * lat_count + lat

    lats = [lat] + [lax.rem(lat + t, lat_count) for t in range(1, lat_count)]
    specs = [spec] + [lax.rem(spec + t, spec_count) for t in range(1, spec_count)]
    others = [(q, b) for b in lats for q in specs][1:]

    def finish(buf, blocks, sem):
        part = buf.at[pl.ds(0, blocks * 16)]
        pltpu.make_async_copy(part, part, sem).wait()

    waves_copy = pltpu.make_async_copy(waves_hbm, waves_ref, local_sem.at[0])
    skip_copy = pltpu.make_async_copy(skip_hbm, skip_ref, local_sem.at[1])
    weight_copy = pltpu.make_async_copy(weight_hbm, weight_ref, local_sem.at[2])
    given_copy = pltpu.make_async_copy(given_hbm, given_ref, local_sem.at[3])
    field_copy = pltpu.make_async_copy(field_ref, field_buf, local_sem.at[4])
    table_move = pltpu.make_async_copy(table_hbm, table_raw, local_sem.at[5])
    table_move.start()
    barrier = pltpu.get_barrier_semaphore()
    for q, b in others:
        pl.semaphore_signal(
            barrier, inc=1, device_id={"spec": q, "lat": b}, device_id_type=MESH
        )
    for copy in (waves_copy, skip_copy, weight_copy, given_copy, field_copy):
        copy.start()

    table_move.wait()
    per_row = WIDE // LANES

    @pl.loop(0, lat_count)
    def _(o):
        for t in range(table_ref.shape[1] * 16 // (pair_dev * LANES)):
            u, v = t // per_row, t % per_row
            if 2 * t < slots:
                both = jnp.concatenate(
                    [table_raw[o, 2 * t].astype(f32), table_raw[o, 2 * t + 1].astype(f32)], axis=1
                )
            else:
                both = jnp.zeros((pair_dev, LANES), f32)
            table_stage[o, u * pair_dev : (u + 1) * pair_dev, v * LANES : (v + 1) * LANES] = both

    table_ref[...] = table_stage[...].reshape(table_ref.shape).astype(bf16)
    pl.semaphore_wait(barrier, dest_count - 1)
    for b in lats[1:]:
        pltpu.make_async_remote_copy(
            src_ref=table_ref.at[pl.ds(b * 16, 16)],
            dst_ref=table_recv.at[pl.ds(lat * 16, 16)],
            send_sem=table_send_sem,
            recv_sem=table_recv_sem,
            device_id={"lat": b},
            device_id_type=MESH,
        ).start()

    own = pl.ds(pl.multiple_of(lat * 16, 16), 16)
    mine = pl.ds(pl.multiple_of(me * 16, 16), 16)
    table_recv[own, :] = table_ref[own, :]
    for copy in (waves_copy, skip_copy, weight_copy):
        copy.wait()

    row8 = lax.broadcasted_iota(jnp.int32, (8, LANES), 0)
    tiles = []
    for tile in range(half // 8):
        wave = jnp.zeros((8, LANES), jnp.int32)
        for row in range(8):
            d, s = divmod(tile * 8 + row, 2)
            wave = jnp.where(row8 == row, waves_ref[d // lat_count, s, d % lat_count], wave)
        tiles.append(wave)
    wave = jnp.concatenate(tiles, axis=0).astype(f32)
    lane_half = lax.broadcasted_iota(jnp.int32, (half, LANES), 1).astype(f32)
    fine = wave * lane_half
    coarse = wave * (lane_half * LANES)
    quarter = length // 4
    cos_b, sin_b = cosine(fine, length), cosine(fine - quarter, length)
    cos_a, sin_a = cosine(coarse, length), cosine(coarse - quarter, length)
    base_c = jnp.concatenate([cos_b, -sin_b], axis=0)
    base_s = jnp.concatenate([sin_b, cos_b], axis=0)
    turn_c = jnp.concatenate([cos_a, cos_a], axis=0)
    turn_s = jnp.concatenate([sin_a, sin_a], axis=0)
    full = length // LANES
    for a in range(pl.cdiv(length, LANES)):
        width = min(LANES, length - a * LANES)
        part = turn_c[:, a : a + 1] * base_c - turn_s[:, a : a + 1] * base_s
        high, low = split(part)
        for n, piece in enumerate((high, low, high, low)):
            waves8[2 * half * n : 2 * half * (n + 1), a * LANES : a * LANES + width] = piece[:, :width]

    given_copy.wait()
    for pair in range(slots // 2):
        both = jnp.concatenate([given_ref[2 * pair], given_ref[2 * pair + 1]], axis=1)
        coeffs[0:columns, pair * LANES : (pair + 1) * LANES] = both
        coeffs[columns : 2 * columns, pair * LANES : (pair + 1) * LANES] = both
    rest = coeffs.shape[1] - slots * KB
    coeffs[:, slots * KB :] = jnp.zeros((2 * columns, rest), bf16)

    field_copy.wait()
    cuts = list(range(0, full * LANES, WIDE)) + [full * LANES]
    cuts = [(b, min(b + WIDE, full * LANES)) for b in cuts[:-1]] + (
        [(full * LANES, length)] if full * LANES < length else []
    )
    total = jnp.zeros((4 * half, LANES), f32)
    for begin, end in cuts:
        high, low = split(field_buf[:, begin:end])
        part = waves8[0 : 4 * half, begin:end]
        total = total + dot(part, high, ACROSS) + dot(part, low, ACROSS)
    fourier = total[: 2 * half] + total[2 * half :]

    lane = lax.broadcasted_iota(jnp.int32, (half, LANES), 1)
    pair_of = (lane // channels) % pair_dev
    weight = jnp.zeros((half, LANES), f32)
    for j in range(pair_dev):
        weight = jnp.where(pair_of == j, weight_ref[j], weight)
    weight = weight * (1.0 / length)

    def butterfly(value):
        turned = pltpu.roll(value, LANES // 2, 1)
        return (turned + jnp.where(lane < LANES // 2, value, -value)) * weight

    folded = [butterfly(fourier[:half]), butterfly(fourier[half:])]
    offsets = [r * spec_count * channels + spec * channels for r in range(2)]
    for pj in range(2 * pair_dev):
        placed = jnp.zeros((half, LANES), f32)
        for r in range(2):
            turned = pltpu.roll(
                folded[r], lax.rem(offsets[r] + (LANES - pj * channels), LANES), 1
            )
            here = (lane >= offsets[r]) & (lane < offsets[r] + channels)
            placed = jnp.where(here, turned, placed)
        stage[pl.ds(pj, half, stride=2 * pair_dev), :] = placed
    fold_send[...] = stage[...].astype(bf16)

    for q, b in others:
        pltpu.make_async_remote_copy(
            src_ref=fold_send.at[pl.ds((q * lat_count + b) * 16, 16)],
            dst_ref=fold_recv.at[pl.ds(me * 16, 16)],
            send_sem=fold_send_sem,
            recv_sem=fold_recv_sem,
            device_id={"spec": q, "lat": b},
            device_id_type=MESH,
        ).start()

    fold_recv[mine, :] = fold_send[mine, :]

    m0, m1 = waves_ref[spec, 0, lat], waves_ref[spec, 1, lat]
    start1 = KB * ((L + KB - m0) >> SHIFT)
    lows, highs = [], []
    for b in range(lat_count):
        for s, (m, start) in enumerate(((m0, 0), (m1, start1))):
            lows.append(jnp.full((2 * pair_dev, LANES), start + KB * skip_ref[b, spec, s, lat]))
            highs.append(jnp.full((2 * pair_dev, LANES), L - m + start))
    lowest = jnp.concatenate(lows, axis=0)
    highest = jnp.concatenate(highs, axis=0)
    rows = lat_count * group
    row_q = lax.broadcasted_iota(jnp.int32, (rows, LANES), 0)
    lane_q = lax.broadcasted_iota(jnp.int32, (rows, LANES), 1)
    parity_ok = (lane_q & 1) == ((row_q // pair_dev) & 1)
    pick_row = lax.broadcasted_iota(jnp.int32, (rows, lat_count * 16), 0)
    pick_col = lax.broadcasted_iota(jnp.int32, (rows, lat_count * 16), 1)
    same_band = (pick_row // group) == (pick_col // 16)

    finish(table_recv, lat_count - 1, table_recv_sem)

    blocks = table_recv[...]
    for u in range(masked.shape[1] // WIDE):
        chosen = same_band & ((pick_col % 16) == u * pair_dev + pick_row % pair_dev)
        pick = jnp.where(chosen, 1.0, 0.0).astype(bf16)
        spread = dot(pick, blocks)
        for v in range(WIDE // LANES):
            at = u * WIDE + v * LANES
            spot = lane_q + at
            keep = parity_ok & (spot >= lowest) & (spot <= highest)
            piece = spread[:, v * LANES : (v + 1) * LANES]
            masked[:, at : at + LANES] = jnp.where(keep, piece, 0.0).astype(bf16)

    synthesis = dot(masked[...], coeffs[...], ACROSS)
    rounded = synthesis.astype(bf16).astype(f32)
    syn_send[...] = jnp.where(lane_q < columns, rounded, synthesis - rounded).astype(bf16)

    for q, b in others:
        pltpu.make_async_remote_copy(
            src_ref=syn_send.at[pl.ds(b * 16, 16)],
            dst_ref=syn_recv.at[pl.ds(me * 16, 16)],
            send_sem=syn_send_sem,
            recv_sem=syn_recv_sem,
            device_id={"spec": q, "lat": b},
            device_id_type=MESH,
        ).start()

    syn_recv[mine, :] = syn_send[own, :]

    finish(fold_recv, dest_count - 1, fold_recv_sem)
    gathered = fold_recv[0:rows, :].astype(f32)
    for q in range(1, spec_count):
        gathered = gathered + fold_recv[q * rows : (q + 1) * rows, :].astype(f32)
    folded_own = gathered.T[:columns].astype(bf16)
    for u in range(masked.shape[1] // WIDE):
        part = dot(folded_own, masked[:, u * WIDE : (u + 1) * WIDE])
        for k in range(u * WIDE // KB, min((u + 1) * WIDE // KB, slots)):
            at = k * KB - u * WIDE
            spectrum_ref[k] = part[:, at : at + KB]

    finish(syn_recv, dest_count - 1, syn_recv_sem)

    received = syn_recv[...].astype(f32)
    stage[...] = received + pltpu.roll(received, LANES // 2, 1)
    back = [jnp.zeros((half, LANES), f32) for _ in range(2)]
    for pj in range(2 * pair_dev):
        value = stage[pl.ds(pj, half, stride=2 * pair_dev), :]
        for r in range(2):
            turned = pltpu.roll(value, lax.rem(LANES + pj * channels - offsets[r], LANES), 1)
            back[r] = jnp.where((lane // channels) == pj, turned, back[r])
    back = jnp.concatenate([butterfly(back[0]), butterfly(back[1])], axis=0)
    high, low = split(jnp.concatenate([back, back], axis=0).T)
    back_ref[...] = jnp.concatenate([high, low], axis=1)

    finish(table_recv, lat_count - 1, table_send_sem)
    finish(fold_recv, dest_count - 1, fold_send_sem)
    finish(syn_recv, dest_count - 1, syn_send_sem)


def stay(array):
    return pltpu.with_memory_space_constraint(array, pltpu.HBM)


def write_kernel(spectrum_in, waves8, back_ref, spectrum_ref, grid_ref, buf, sem):
    length = grid_ref.shape[1]
    copies = [pltpu.make_async_copy(spectrum_in, spectrum_ref, sem.at[0])]
    copies[0].start()
    back = back_ref[...]
    parts = sem.shape[0] - 1
    for n in range(parts):
        begin = n * WIDE
        end = length if n == parts - 1 else begin + WIDE
        buf[:, begin:end] = dot(back, waves8[:, begin:end])
        copy = pltpu.make_async_copy(
            buf.at[:, pl.ds(begin, end - begin)],
            grid_ref.at[:, pl.ds(begin, end - begin)],
            sem.at[1 + n],
        )
        copy.start()
        copies.append(copy)
    for copy in copies:
        copy.wait()


def on_device(
    lat_count, spec_count, field_grid, quad_weight, owner_waves, skip_blocks, legendre_table, given_spectrum
):
    hemispheres, pair_dev, channels, length = field_grid.shape
    slots = given_spectrum.shape[2]
    columns = 2 * given_spectrum.shape[4]
    dest_count = lat_count * spec_count
    rows = lat_count * 4 * pair_dev
    quarters = 16 // pair_dev
    half = 2 * dest_count
    f32, bf16 = jnp.float32, jnp.bfloat16
    vmem = pl.BlockSpec(memory_space=pltpu.VMEM)
    dma = pltpu.SemaphoreType.DMA
    hbm = pl.BlockSpec(memory_space=pltpu.HBM)
    spectrum, wave_table, back = pl.pallas_call(
        functools.partial(kernel, lat_count, spec_count),
        out_shape=(
            jax.ShapeDtypeStruct((slots, columns, KB), f32),
            jax.ShapeDtypeStruct((8 * half, length), bf16),
            jax.ShapeDtypeStruct((LANES, 8 * half), bf16),
        ),
        in_specs=[hbm] * 6,
        out_specs=(vmem,) * 3,
        scratch_shapes=[
            pltpu.SMEM((spec_count, 2, lat_count), jnp.int32),
            pltpu.SMEM((lat_count, spec_count, 2, lat_count), jnp.int32),
            pltpu.SMEM((pair_dev,), f32),
            pltpu.VMEM((slots, columns, KB), bf16),
            pltpu.VMEM((lat_count, slots, pair_dev, KB), bf16),
            pltpu.VMEM((lat_count, 16, WIDE), f32),
            pltpu.VMEM((lat_count * 16, WIDE), bf16),
            pltpu.VMEM((LANES, length), f32),
            pltpu.VMEM((lat_count * 16, WIDE), bf16),
            pltpu.VMEM((dest_count * 16, LANES), f32),
            pltpu.VMEM((dest_count * 16, LANES), bf16),
            pltpu.VMEM((spec_count * rows, LANES), bf16),
            pltpu.VMEM((rows, LANES), bf16),
            pltpu.VMEM((dest_count * 16, LANES), bf16),
            pltpu.VMEM((rows, quarters * WIDE), bf16),
            pltpu.VMEM((2 * columns, quarters * WIDE), bf16),
            dma((6,)),
            dma,
            dma,
            dma,
            dma,
            dma,
            dma,
        ],
        compiler_params=pltpu.CompilerParams(
            collective_id=0, has_side_effects=True, vmem_limit_bytes=32 * 2**20
        ),
        name="transform",
    )(
        stay(jnp.transpose(owner_waves, (0, 2, 1))),
        stay(jnp.transpose(skip_blocks, (0, 1, 3, 2))),
        stay(quad_weight),
        stay(field_grid.reshape(LANES, length)),
        stay(legendre_table[0]),
        stay(given_spectrum.reshape(slots, columns, KB)),
    )
    spectrum, back_grid = pl.pallas_call(
        write_kernel,
        out_shape=(
            jax.ShapeDtypeStruct((slots, columns, KB), f32),
            jax.ShapeDtypeStruct((LANES, length), f32),
        ),
        in_specs=[vmem] * 3,
        out_specs=(hbm, hbm),
        scratch_shapes=[pltpu.VMEM((LANES, length), f32), dma((1 + length // WIDE,))],
        compiler_params=pltpu.CompilerParams(vmem_limit_bytes=16 * 2**20),
        name="write_out",
    )(spectrum, wave_table, back)
    return (spectrum.reshape(given_spectrum.shape), back_grid.reshape(field_grid.shape))


def solution(mesh):
    lat_count, spec_count = mesh.shape["lat"], mesh.shape["spec"]

    def body(*args):
        return on_device(lat_count, spec_count, *args)

    return jax.shard_map(
        body,
        mesh=mesh,
        in_specs=(
            P(None, "lat", ("group", "spec"), None),
            P("lat"),
            P(),
            P(),
            P("spec", None, None, "lat", None),
            P("spec", "lat", None, None, "group", None),
        ),
        out_specs=(
            P("spec", "lat", None, None, "group", None),
            P(None, "lat", ("group", "spec"), None),
        ),
        check_vma=False,
    )
```

```python
import functools
import math

import jax
import jax.numpy as jnp
from jax import lax
from jax.experimental import pallas as pl
from jax.experimental.pallas import tpu as pltpu
from jax.sharding import PartitionSpec as P

L = 1800
KB = 64
SHIFT = 6
LANES = 128
WIDE = 512
MESH = pl.DeviceIdType.MESH
ACROSS = (((1,), (1,)), ((), ()))
PLAIN = (((1,), (0,)), ((), ()))


def dot(a, b, dims=PLAIN):
    return lax.dot_general(a, b, dims, preferred_element_type=jnp.float32)


def cosine(phase, length):
    turns = jnp.floor(phase * (1.0 / length) + 0.5)
    angle = (phase - turns * length) * (2.0 * math.pi / length)
    z = angle * angle
    total = jnp.full_like(z, 1.0 / math.factorial(20))
    for n in range(18, -1, -2):
        sign = -1.0 if (n // 2) % 2 else 1.0
        total = total * z + sign / math.factorial(n)
    return total


def split(value):
    high = value.astype(jnp.bfloat16)
    return high, (value - high.astype(jnp.float32)).astype(jnp.bfloat16)


def kernel(
    lat_count,
    spec_count,
    waves_hbm,
    skip_hbm,
    weight_hbm,
    field_ref,
    table_hbm,
    given_hbm,
    spectrum_ref,
    waves8,
    back_ref,
    waves_ref,
    skip_ref,
    weight_ref,
    given_ref,
    table_raw,
    table_stage,
    table_ref,
    field_buf,
    table_recv,
    stage,
    fold_send,
    fold_recv,
    syn_send,
    syn_recv,
    masked,
    coeffs,
    local_sem,
    table_send_sem,
    table_recv_sem,
    fold_send_sem,
    fold_recv_sem,
    syn_send_sem,
    syn_recv_sem,
):
    f32, bf16 = jnp.float32, jnp.bfloat16
    length = field_ref.shape[1]
    pair_dev = weight_ref.shape[0]
    channels = LANES // (2 * pair_dev)
    slots = given_ref.shape[0]
    columns = given_ref.shape[1]
    dest_count = lat_count * spec_count
    half = 2 * dest_count
    group = 4 * pair_dev
    lat = lax.axis_index("lat")
    spec = lax.axis_index("spec")
    me = spec * lat_count + lat

    lats = [lat] + [lax.rem(lat + t, lat_count) for t in range(1, lat_count)]
    specs = [spec] + [lax.rem(spec + t, spec_count) for t in range(1, spec_count)]
    others = [(q, b) for b in lats for q in specs][1:]

    def finish(buf, blocks, sem):
        part = buf.at[pl.ds(0, blocks * 16)]
        pltpu.make_async_copy(part, part, sem).wait()

    waves_copy = pltpu.make_async_copy(waves_hbm, waves_ref, local_sem.at[0])
    skip_copy = pltpu.make_async_copy(skip_hbm, skip_ref, local_sem.at[1])
    weight_copy = pltpu.make_async_copy(weight_hbm, weight_ref, local_sem.at[2])
    given_copy = pltpu.make_async_copy(given_hbm, given_ref, local_sem.at[3])
    field_copy = pltpu.make_async_copy(field_ref, field_buf, local_sem.at[4])
    table_move = pltpu.make_async_copy(table_hbm, table_raw, local_sem.at[5])
    table_move.start()
    barrier = pltpu.get_barrier_semaphore()
    for q, b in others:
        pl.semaphore_signal(
            barrier, inc=1, device_id={"spec": q, "lat": b}, device_id_type=MESH
        )
    for copy in (waves_copy, skip_copy, weight_copy, given_copy, field_copy):
        copy.start()

    table_move.wait()
    per_row = WIDE // LANES

    @pl.loop(0, lat_count)
    def _(o):
        for t in range(table_ref.shape[1] * 16 // (pair_dev * LANES)):
            u, v = t // per_row, t % per_row
            if 2 * t < slots:
                both = jnp.concatenate(
                    [table_raw[o, 2 * t].astype(f32), table_raw[o, 2 * t + 1].astype(f32)], axis=1
                )
            else:
                both = jnp.zeros((pair_dev, LANES), f32)
            table_stage[o, u * pair_dev : (u + 1) * pair_dev, v * LANES : (v + 1) * LANES] = both

    table_ref[...] = table_stage[...].reshape(table_ref.shape).astype(bf16)
    pl.semaphore_wait(barrier, dest_count - 1)
    for b in lats[1:]:
        pltpu.make_async_remote_copy(
            src_ref=table_ref.at[pl.ds(b * 16, 16)],
            dst_ref=table_recv.at[pl.ds(lat * 16, 16)],
            send_sem=table_send_sem,
            recv_sem=table_recv_sem,
            device_id={"lat": b},
            device_id_type=MESH,
        ).start()

    own = pl.ds(pl.multiple_of(lat * 16, 16), 16)
    mine = pl.ds(pl.multiple_of(me * 16, 16), 16)
    table_recv[own, :] = table_ref[own, :]
    for copy in (waves_copy, skip_copy, weight_copy):
        copy.wait()

    row8 = lax.broadcasted_iota(jnp.int32, (8, LANES), 0)
    tiles = []
    for tile in range(half // 8):
        wave = jnp.zeros((8, LANES), jnp.int32)
        for row in range(8):
            d, s = divmod(tile * 8 + row, 2)
            wave = jnp.where(row8 == row, waves_ref[d // lat_count, s, d % lat_count], wave)
        tiles.append(wave)
    wave = jnp.concatenate(tiles, axis=0).astype(f32)
    lane_half = lax.broadcasted_iota(jnp.int32, (half, LANES), 1).astype(f32)
    fine = wave * lane_half
    coarse = wave * (lane_half * LANES)
    quarter = length // 4
    cos_b, sin_b = cosine(fine, length), cosine(fine - quarter, length)
    cos_a, sin_a = cosine(coarse, length), cosine(coarse - quarter, length)
    base_c = jnp.concatenate([cos_b, -sin_b], axis=0)
    base_s = jnp.concatenate([sin_b, cos_b], axis=0)
    turn_c = jnp.concatenate([cos_a, cos_a], axis=0)
    turn_s = jnp.concatenate([sin_a, sin_a], axis=0)
    full = length // LANES
    for a in range(pl.cdiv(length, LANES)):
        width = min(LANES, length - a * LANES)
        part = turn_c[:, a : a + 1] * base_c - turn_s[:, a : a + 1] * base_s
        high, low = split(part)
        for n, piece in enumerate((high, low, high, low)):
            waves8[2 * half * n : 2 * half * (n + 1), a * LANES : a * LANES + width] = piece[:, :width]

    given_copy.wait()
    for pair in range(slots // 2):
        both = jnp.concatenate([given_ref[2 * pair], given_ref[2 * pair + 1]], axis=1)
        coeffs[0:columns, pair * LANES : (pair + 1) * LANES] = both
        coeffs[columns : 2 * columns, pair * LANES : (pair + 1) * LANES] = both
    rest = coeffs.shape[1] - slots * KB
    coeffs[:, slots * KB :] = jnp.zeros((2 * columns, rest), bf16)

    field_copy.wait()
    cuts = list(range(0, full * LANES, WIDE)) + [full * LANES]
    cuts = [(b, min(b + WIDE, full * LANES)) for b in cuts[:-1]] + (
        [(full * LANES, length)] if full * LANES < length else []
    )
    total = jnp.zeros((4 * half, LANES), f32)
    for begin, end in cuts:
        high, low = split(field_buf[:, begin:end])
        part = waves8[0 : 4 * half, begin:end]
        total = total + dot(part, high, ACROSS) + dot(part, low, ACROSS)
    fourier = total[: 2 * half] + total[2 * half :]

    m0, m1 = waves_ref[spec, 0, lat], waves_ref[spec, 1, lat]
    start1 = KB * ((L + KB - m0) >> SHIFT)
    lows, highs = [], []
    for b in range(lat_count):
        for s, (m, start) in enumerate(((m0, 0), (m1, start1))):
            lows.append(jnp.full((2 * pair_dev, LANES), start + KB * skip_ref[b, spec, s, lat]))
            highs.append(jnp.full((2 * pair_dev, LANES), L - m + start))
    lowest = jnp.concatenate(lows, axis=0)
    highest = jnp.concatenate(highs, axis=0)
    rows = lat_count * group
    row_q = lax.broadcasted_iota(jnp.int32, (rows, LANES), 0)
    lane_q = lax.broadcasted_iota(jnp.int32, (rows, LANES), 1)
    parity_ok = (lane_q & 1) == ((row_q // pair_dev) & 1)
    pick_row = lax.broadcasted_iota(jnp.int32, (rows, lat_count * 16), 0)
    pick_col = lax.broadcasted_iota(jnp.int32, (rows, lat_count * 16), 1)
    same_band = (pick_row // group) == (pick_col // 16)

    finish(table_recv, lat_count - 1, table_recv_sem)

    blocks = table_recv[...]
    for u in range(masked.shape[1] // WIDE):
        chosen = same_band & ((pick_col % 16) == u * pair_dev + pick_row % pair_dev)
        pick = jnp.where(chosen, 1.0, 0.0).astype(bf16)
        spread = dot(pick, blocks)
        for v in range(WIDE // LANES):
            at = u * WIDE + v * LANES
            spot = lane_q + at
            keep = parity_ok & (spot >= lowest) & (spot <= highest)
            piece = spread[:, v * LANES : (v + 1) * LANES]
            masked[:, at : at + LANES] = jnp.where(keep, piece, 0.0).astype(bf16)

    synthesis = dot(masked[...], coeffs[...], ACROSS)
    rounded = synthesis.astype(bf16).astype(f32)
    syn_send[...] = jnp.where(lane_q < columns, rounded, synthesis - rounded).astype(bf16)

    for q, b in others:
        pltpu.make_async_remote_copy(
            src_ref=syn_send.at[pl.ds(b * 16, 16)],
            dst_ref=syn_recv.at[pl.ds(me * 16, 16)],
            send_sem=syn_send_sem,
            recv_sem=syn_recv_sem,
            device_id={"spec": q, "lat": b},
            device_id_type=MESH,
        ).start()

    syn_recv[mine, :] = syn_send[own, :]

    lane = lax.broadcasted_iota(jnp.int32, (half, LANES), 1)
    pair_of = (lane // channels) % pair_dev
    weight = jnp.zeros((half, LANES), f32)
    for j in range(pair_dev):
        weight = jnp.where(pair_of == j, weight_ref[j], weight)
    weight = weight * (1.0 / length)

    def butterfly(value):
        turned = pltpu.roll(value, LANES // 2, 1)
        return (turned + jnp.where(lane < LANES // 2, value, -value)) * weight

    folded = [butterfly(fourier[:half]), butterfly(fourier[half:])]
    offsets = [r * spec_count * channels + spec * channels for r in range(2)]
    for pj in range(2 * pair_dev):
        placed = jnp.zeros((half, LANES), f32)
        for r in range(2):
            turned = pltpu.roll(
                folded[r], lax.rem(offsets[r] + (LANES - pj * channels), LANES), 1
            )
            here = (lane >= offsets[r]) & (lane < offsets[r] + channels)
            placed = jnp.where(here, turned, placed)
        stage[pl.ds(pj, half, stride=2 * pair_dev), :] = placed
    fold_send[...] = stage[...].astype(bf16)

    for q, b in others:
        pltpu.make_async_remote_copy(
            src_ref=fold_send.at[pl.ds((q * lat_count + b) * 16, 16)],
            dst_ref=fold_recv.at[pl.ds(me * 16, 16)],
            send_sem=fold_send_sem,
            recv_sem=fold_recv_sem,
            device_id={"spec": q, "lat": b},
            device_id_type=MESH,
        ).start()

    fold_recv[mine, :] = fold_send[mine, :]

    finish(syn_recv, dest_count - 1, syn_recv_sem)

    received = syn_recv[...].astype(f32)
    stage[...] = received + pltpu.roll(received, LANES // 2, 1)
    back = [jnp.zeros((half, LANES), f32) for _ in range(2)]
    for pj in range(2 * pair_dev):
        value = stage[pl.ds(pj, half, stride=2 * pair_dev), :]
        for r in range(2):
            turned = pltpu.roll(value, lax.rem(LANES + pj * channels - offsets[r], LANES), 1)
            back[r] = jnp.where((lane // channels) == pj, turned, back[r])
    back = jnp.concatenate([butterfly(back[0]), butterfly(back[1])], axis=0)
    high, low = split(jnp.concatenate([back, back], axis=0).T)
    back_ref[...] = jnp.concatenate([high, low], axis=1)

    finish(fold_recv, dest_count - 1, fold_recv_sem)
    gathered = fold_recv[0:rows, :].astype(f32)
    for q in range(1, spec_count):
        gathered = gathered + fold_recv[q * rows : (q + 1) * rows, :].astype(f32)
    folded_own = gathered.T[:columns].astype(bf16)
    for u in range(masked.shape[1] // WIDE):
        part = dot(folded_own, masked[:, u * WIDE : (u + 1) * WIDE])
        for k in range(u * WIDE // KB, min((u + 1) * WIDE // KB, slots)):
            at = k * KB - u * WIDE
            spectrum_ref[k] = part[:, at : at + KB]

    finish(table_recv, lat_count - 1, table_send_sem)
    finish(fold_recv, dest_count - 1, fold_send_sem)
    finish(syn_recv, dest_count - 1, syn_send_sem)


def stay(array):
    return pltpu.with_memory_space_constraint(array, pltpu.HBM)


def write_kernel(spectrum_in, waves8, back_ref, spectrum_ref, grid_ref, buf, sem):
    length = grid_ref.shape[1]
    copies = [pltpu.make_async_copy(spectrum_in, spectrum_ref, sem.at[0])]
    copies[0].start()
    back = back_ref[...]
    parts = sem.shape[0] - 1
    for n in range(parts):
        begin = n * WIDE
        end = length if n == parts - 1 else begin + WIDE
        buf[:, begin:end] = dot(back, waves8[:, begin:end])
        copy = pltpu.make_async_copy(
            buf.at[:, pl.ds(begin, end - begin)],
            grid_ref.at[:, pl.ds(begin, end - begin)],
            sem.at[1 + n],
        )
        copy.start()
        copies.append(copy)
    for copy in copies:
        copy.wait()


def on_device(
    lat_count, spec_count, field_grid, quad_weight, owner_waves, skip_blocks, legendre_table, given_spectrum
):
    hemispheres, pair_dev, channels, length = field_grid.shape
    slots = given_spectrum.shape[2]
    columns = 2 * given_spectrum.shape[4]
    dest_count = lat_count * spec_count
    rows = lat_count * 4 * pair_dev
    quarters = 16 // pair_dev
    half = 2 * dest_count
    f32, bf16 = jnp.float32, jnp.bfloat16
    vmem = pl.BlockSpec(memory_space=pltpu.VMEM)
    dma = pltpu.SemaphoreType.DMA
    hbm = pl.BlockSpec(memory_space=pltpu.HBM)
    spectrum, wave_table, back = pl.pallas_call(
        functools.partial(kernel, lat_count, spec_count),
        out_shape=(
            jax.ShapeDtypeStruct((slots, columns, KB), f32),
            jax.ShapeDtypeStruct((8 * half, length), bf16),
            jax.ShapeDtypeStruct((LANES, 8 * half), bf16),
        ),
        in_specs=[hbm] * 6,
        out_specs=(vmem,) * 3,
        scratch_shapes=[
            pltpu.SMEM((spec_count, 2, lat_count), jnp.int32),
            pltpu.SMEM((lat_count, spec_count, 2, lat_count), jnp.int32),
            pltpu.SMEM((pair_dev,), f32),
            pltpu.VMEM((slots, columns, KB), bf16),
            pltpu.VMEM((lat_count, slots, pair_dev, KB), bf16),
            pltpu.VMEM((lat_count, 16, WIDE), f32),
            pltpu.VMEM((lat_count * 16, WIDE), bf16),
            pltpu.VMEM((LANES, length), f32),
            pltpu.VMEM((lat_count * 16, WIDE), bf16),
            pltpu.VMEM((dest_count * 16, LANES), f32),
            pltpu.VMEM((dest_count * 16, LANES), bf16),
            pltpu.VMEM((spec_count * rows, LANES), bf16),
            pltpu.VMEM((rows, LANES), bf16),
            pltpu.VMEM((dest_count * 16, LANES), bf16),
            pltpu.VMEM((rows, quarters * WIDE), bf16),
            pltpu.VMEM((2 * columns, quarters * WIDE), bf16),
            dma((6,)),
            dma,
            dma,
            dma,
            dma,
            dma,
            dma,
        ],
        compiler_params=pltpu.CompilerParams(
            collective_id=0, has_side_effects=True, vmem_limit_bytes=32 * 2**20
        ),
        name="transform",
    )(
        stay(jnp.transpose(owner_waves, (0, 2, 1))),
        stay(jnp.transpose(skip_blocks, (0, 1, 3, 2))),
        stay(quad_weight),
        stay(field_grid.reshape(LANES, length)),
        stay(legendre_table[0]),
        stay(given_spectrum.reshape(slots, columns, KB)),
    )
    spectrum, back_grid = pl.pallas_call(
        write_kernel,
        out_shape=(
            jax.ShapeDtypeStruct((slots, columns, KB), f32),
            jax.ShapeDtypeStruct((LANES, length), f32),
        ),
        in_specs=[vmem] * 3,
        out_specs=(hbm, hbm),
        scratch_shapes=[pltpu.VMEM((LANES, length), f32), dma((1 + length // WIDE,))],
        compiler_params=pltpu.CompilerParams(vmem_limit_bytes=16 * 2**20),
        name="write_out",
    )(spectrum, wave_table, back)
    return (spectrum.reshape(given_spectrum.shape), back_grid.reshape(field_grid.shape))


def solution(mesh):
    lat_count, spec_count = mesh.shape["lat"], mesh.shape["spec"]

    def body(*args):
        return on_device(lat_count, spec_count, *args)

    return jax.shard_map(
        body,
        mesh=mesh,
        in_specs=(
            P(None, "lat", ("group", "spec"), None),
            P("lat"),
            P(),
            P(),
            P("spec", None, None, "lat", None),
            P("spec", "lat", None, None, "group", None),
        ),
        out_specs=(
            P("spec", "lat", None, None, "group", None),
            P(None, "lat", ("group", "spec"), None),
        ),
        check_vma=False,
    )
```
